512 devices in a mesh: prefix: 16 (over z_lo, y), ctx: 4 (over z_hi), kvh: 8 (over x, core).
Axes of the slice: x: 4, y: 8, z: 8 (z_hi: 4, z_lo: 2; z = z_hi * 2 + z_lo), core: 2. Of those that a mesh axis runs over, the one named last changes fastest.
Arguments:
- queries: bfloat16 [1024, 8192], P(('prefix', 'ctx'), 'kvh'), may hold values from -6.5 to 6.5
- prefix_ids: int32 [1024, 1], P(('prefix', 'ctx')), may hold values from 0 to 15; in each aligned block of 16 rows (0 to 15, 16 to 31, ...) at most 2 rows name the same one
- keys: bfloat16 [16, 16384, 1024], P('prefix', 'ctx', 'kvh'), may hold values from -6 to 6
- values: bfloat16 [16, 16384, 1024], P('prefix', 'ctx', 'kvh'), may hold values from -6 to 6
Outputs:
- attended: bfloat16 [1024, 8192], P(('prefix', 'ctx'), 'kvh')
The draws below stay inside these ranges and needn't reach their ends.
Inputs may be any that keep to these rules, and one draw needn't show every extreme that they name: `prefix_ids`: in each aligned block of 16 rows (one request device's requests) no prefix is named by more than 2 rows, a bound that some block reaches.
All inputs are finite; a program needn't handle non-finite values.
Results may differ from the reference program's by a relative error of at most 0.0048.
Values may be sent and summed in bfloat16 or wider, within the bound.
A program may use at most 64 MiB of HBM per device.

```python
import math
import jax
import jax.numpy as jnp
import numpy as np
from jax import lax

H = 64
KVH = 8
DH = 128
SEND_CAP = 2
GROUP = 8
REQ_DEV = 16
REQUESTS = 1024
SLOTS = 128
LEN = 16384
N_PREFIX = 16
N_CTX = 4


def draw_queries(key, part):
    key = jax.random.fold_in(key, 11)
    filled = jnp.clip(jax.random.normal(key, (REQUESTS, H, DH), jnp.float32), -6.0, 6.0)
    return filled.reshape(REQUESTS, H * DH).astype(jnp.bfloat16)


def draw_keys(key, part):
    key = jax.random.fold_in(key, 12)
    filled = jnp.clip(jax.random.normal(key, (N_PREFIX, LEN, KVH, DH), jnp.float32), -6.0, 6.0)
    return filled.reshape(N_PREFIX, LEN, KVH * DH).astype(jnp.bfloat16)


def steps_of(rng, shape, cuts, smallest, largest):
    factor_of = 1.0
    for dim, parts in cuts:
        draws = jax.random.uniform(jax.random.fold_in(jax.random.fold_in(rng, 6), dim), (parts,), jnp.float32, smallest / len(cuts), largest / len(cuts))
        factor_of = factor_of * jnp.repeat(jnp.exp(draws), shape[dim] // parts).reshape((-1,) + (1,) * (len(shape) - 1 - dim))
    return factor_of


def deal_out(key, own, number, rows, count, top, most, skew):
    sequence = jax.random.permutation(key, count)
    crowded, ordinary = load_shares(count, rows * top, most, skew, True), load_shares(count, rows * top, most, skew, False)
    places = jnp.arange(count)

    def named(sizes, offset_by):
        used = int((sizes > 0).sum())
        fixed = max(1, used // 4)
        moved = fixed + (places - fixed + offset_by * (used - fixed)) % max(1, count - fixed)
        return jnp.zeros((count,), jnp.int32).at[sequence[jnp.where(places < fixed, places, moved)]].set(jnp.asarray(sizes, jnp.int32))

    sizes = jnp.where(number % 4 == 0, named(crowded, number // 4), named(ordinary, number - number // 4 - 1))
    mixed = jax.random.permutation(jax.random.fold_in(own, 3), count)
    source_of, taker = mixed[0:count // 2 * 2:2], mixed[1:count // 2 * 2:2]
    margin = jnp.minimum(sizes[source_of] - 1, most - sizes[taker]) // 2
    margin = jnp.where((source_of == sequence[0]) | (taker == sequence[0]) | (sizes[taker] == 0), 0, jnp.maximum(margin, 0))
    moved = jax.random.randint(jax.random.fold_in(own, 4), (count // 2,), 0, 1 << 20) % (margin + 1)
    sizes = sizes.at[source_of].add(-moved).at[taker].add(moved)
    labels = jnp.searchsorted(jnp.cumsum(sizes), jnp.arange(rows * top), side="right").astype(jnp.int32)
    listing = labels.reshape(top, rows).T
    listing = listing[jax.random.permutation(jax.random.fold_in(own, 1), rows)]
    offset_by = jax.random.randint(jax.random.fold_in(own, 2), (rows, 1), 0, top)
    return jnp.take_along_axis(listing, (jnp.arange(top)[None, :] + offset_by) % top, axis=1)


def load_shares(count, total, reach, skew, full):
    loads = [(1 << 20) // math.isqrt(grade ** skew) + 1 for grade in range(1, count + 1)]
    largest = reach if full else min(reach, max(-(-total // count), total * loads[0] // sum(loads)))
    least = 1 if total - largest >= count - 1 else 0
    counts, spare = [largest] + [least] * (count - 1), total - largest - least * (count - 1)
    while spare > 0:
        candidates = [i for i in range(1, count) if counts[i] < largest] or [i for i in range(1, count) if counts[i] < reach]
        whole, remaining = sum([loads[i] for i in candidates]), spare
        for i in candidates:
            more = min(reach - counts[i], max(1, remaining * loads[i] // whole), spare)
            counts[i] = counts[i] + more
            spare = spare - more
    return np.array(counts)


def noise(stream_key, dims, width, reach, shards=(), held_as=jnp.bfloat16):
    entries = jax.random.normal(stream_key, dims, jnp.float32) * width
    if len(shards) > 0:
        entries = steps_of(stream_key, dims, shards, -0.22, 0.18) * entries
    return jnp.clip(entries, min=-reach, max=reach).astype(held_as)


def setup_inputs(seed: int = 0) -> dict:
    streams_of = jax.random.split(jax.random.key(seed), 5)
    queries = draw_queries(jax.random.fold_in(streams_of[4], 71), 0)
    prefix_ids_keys = jax.random.split(jax.random.fold_in(streams_of[1], 1), REQUESTS // REQ_DEV)
    prefix_ids_turns = jax.random.permutation(jax.random.fold_in(streams_of[1], 3), REQUESTS // REQ_DEV)
    prefix_ids = jax.vmap(lambda own, number: deal_out(jax.random.fold_in(streams_of[1], 2), own, number, REQ_DEV, N_PREFIX, 1, SEND_CAP, 2))(prefix_ids_keys, prefix_ids_turns).reshape((REQUESTS, 1))
    keys = draw_keys(jax.random.fold_in(streams_of[4], 71), 0)
    values = noise(streams_of[3], (N_PREFIX, LEN, KVH * DH), 1.0, 6.0, ((0, 16), (1, 4), (2, 8)))
    return {"queries": queries, "prefix_ids": prefix_ids, "keys": keys, "values": values}


def reference(queries, prefix_ids, keys, values):
    n_dev = N_PREFIX * N_CTX
    per_dev = queries.shape[0] // n_dev
    pref_rows = prefix_ids[:, 0].reshape(n_dev, per_dev)
    same_pref = pref_rows[:, :, None] == pref_rows[:, None, :]
    earlier = jnp.arange(per_dev)[:, None] > jnp.arange(per_dev)[None, :]
    slot_rank = jnp.sum(same_pref & earlier[None], axis=2).astype(jnp.int32)
    device = jnp.arange(n_dev).astype(jnp.int32)
    src_pre = device // N_CTX
    src_ctx = device % N_CTX
    slot_pos = (((src_ctx * N_PREFIX + src_pre)[:, None] * SEND_CAP) + slot_rank).reshape(-1).astype(jnp.int32)
    group_of = pref_rows.reshape(-1).astype(jnp.int32)
    buffer = jnp.zeros((N_PREFIX, SLOTS, H * DH), jnp.bfloat16).at[group_of, slot_pos].set(queries)
    inv_root = DH ** -0.5

    def one_pair(pair_index):
        grp = pair_index // KVH
        head = pair_index % KVH
        group_q = lax.dynamic_index_in_dim(buffer, grp, 0, keepdims=False).reshape(SLOTS, KVH, GROUP, DH)
        head_q = lax.dynamic_index_in_dim(group_q, head, 1, keepdims=False)
        group_k = lax.dynamic_index_in_dim(keys, grp, 0, keepdims=False).reshape(LEN, KVH, DH)
        group_v = lax.dynamic_index_in_dim(values, grp, 0, keepdims=False).reshape(LEN, KVH, DH)
        head_k = lax.dynamic_index_in_dim(group_k, head, 1, keepdims=False)
        head_v = lax.dynamic_index_in_dim(group_v, head, 1, keepdims=False)
        score = jnp.einsum("sed,td->set", head_q.astype(jnp.float32), head_k.astype(jnp.float32)) * inv_root
        top = jnp.max(score, axis=-1)
        expo = jnp.exp(score - top[..., None])
        denom = jnp.sum(expo, axis=-1)
        weights = lax.optimization_barrier(expo.astype(jnp.bfloat16)).astype(jnp.float32)
        numer = jnp.einsum("set,td->sed", weights, head_v.astype(jnp.float32))
        return (numer / denom[..., None]).astype(jnp.bfloat16)

    result = lax.map(one_pair, jnp.arange(N_PREFIX * KVH).astype(jnp.int32))
    result = result.reshape(N_PREFIX, KVH, SLOTS, GROUP, DH)
    result = jnp.transpose(result, (0, 2, 1, 3, 4)).reshape(N_PREFIX, SLOTS, H * DH)
    return result[group_of, slot_pos]
```

```python
import functools
import math

import jax
import jax.numpy as jnp
from jax import lax
from jax.experimental import pallas as pl
from jax.experimental.pallas import tpu as pltpu
from jax.sharding import PartitionSpec as P

DH = 128
SEND_CAP = 2
GROUP = 8
VMEM_LIMIT = 63 * 1024 * 1024
LANES = 128
PIECE = 512
N_CHUNKS = 4
MSG = SEND_CAP * GROUP


def iota(shape, dim):
    return lax.broadcasted_iota(jnp.int32, shape, dim)


def slot_targets(ids_ref):
    n_req = ids_ref.shape[1]
    lane_req = iota((n_req, LANES), 1) % n_req
    row_req = iota((n_req, LANES), 0)
    row = jnp.concatenate([ids_ref[...]] * (LANES // n_req), axis=1)
    col = jnp.sum(jnp.where(iota((n_req, LANES), 1) == row_req, row, 0), axis=1, keepdims=True)
    same = col == row
    rank_row = jnp.sum(jnp.where(same & (row_req < lane_req), 1, 0), axis=0, keepdims=True)
    first = iota((n_req, LANES), 1) < row_req
    rank_col = jnp.sum(jnp.where(same & first, 1, 0), axis=1, keepdims=True)
    return row * SEND_CAP + rank_row, col * SEND_CAP + rank_col


def prefix_order(n_pre):
    side = n_pre // 2
    fours = [[0, side, 1, -1]]
    rest = [[side + 1, side - 1, 2, -2]]
    for far in range(2, side // 2):
        rest.append([side + far, side - far, far + 1, -far - 1])
    rest[-1][-1] = side + side // 2
    order = [step % n_pre for four in fours + rest[1:] + rest[:1] for step in four]
    assert sorted(order) == list(range(n_pre))
    return order


def kernel(
    n_pre, n_ctx, block_len, queries_hbm, ids_hbm, keys, values, out,
    queries, ids, outgoing, q_in, k_raw, v_ones, scores, acc, part, stat, part_in, stat_in,
    load_sem, q_send, q_recv, part_send, part_recv, stat_send, stat_recv,
):
    n_req, features = queries.shape
    ctx_len = keys.shape[1]
    rows = n_pre * MSG
    chunk_rows = n_pre * n_ctx * MSG // N_CHUNKS
    per_tile = LANES // MSG
    pre = lax.axis_index("prefix")
    ctx = lax.axis_index("ctx")
    log_scale = DH ** (-0.5) * math.log2(math.e)

    kvh, n_kvh = lax.axis_index("kvh"), lax.axis_size("kvh")
    pre_at = [lax.rem(pre + step, n_pre) for step in range(n_pre)]
    pre_base = [to * (n_ctx * n_kvh) + kvh for to in pre_at]
    ctx_base = [lax.rem(ctx + off, n_ctx) * n_kvh for off in range(n_ctx)]

    order = prefix_order(n_pre)
    slots = [(step, off) for step in order for off in range(n_ctx)]
    n_slots = len(slots)
    per_chunk = n_slots // N_CHUNKS

    loads = [
        pltpu.make_async_copy(ids_hbm, ids, load_sem.at[2]),
        pltpu.make_async_copy(queries_hbm, queries, load_sem.at[3]),
        pltpu.make_async_copy(keys.at[0], k_raw, load_sem.at[0]),
        pltpu.make_async_copy(values.at[0], v_ones.at[:, pl.ds(0, DH)], load_sem.at[1]),
    ]
    for copy in loads:
        copy.start()
    barrier = pltpu.get_barrier_semaphore()

    for off in range(n_ctx):
        for step in range(n_pre):
            if off or step:
                pl.semaphore_signal(
                    barrier, inc=1, device_id=pre_base[step] + ctx_base[off], device_id_type=pl.DeviceIdType.LOGICAL
                )
    v_ones[:, DH:] = jnp.ones((ctx_len, DH), jnp.bfloat16)
    for copy in loads[:2]:
        copy.wait()

    target_row, target_col = slot_targets(ids)
    r = iota((rows, LANES), 0)
    lane = iota((rows, LANES), 1)
    place = (jnp.broadcast_to(target_row, (rows, LANES)) == r // GROUP) & (r % GROUP == lane // n_req)
    by_head = jnp.concatenate([queries[:, e * DH:(e + 1) * DH] for e in range(GROUP)], axis=0)
    outgoing[...] = jnp.dot(
        jnp.where(place, 1.0, 0.0).astype(jnp.bfloat16), by_head, preferred_element_type=jnp.float32
    ).astype(jnp.bfloat16).reshape(n_pre, MSG, DH)

    pl.semaphore_wait(barrier, n_pre * n_ctx - 1)

    pltpu.make_async_copy(outgoing.at[pre], q_in.at[0], q_recv.at[0]).start()
    for slot, (step, off) in enumerate(slots):
        if slot:
            back, away = (n_pre - step) % n_pre, (n_ctx - off) % n_ctx
            pltpu.make_async_remote_copy(
                src_ref=outgoing.at[pre_at[back]], dst_ref=q_in.at[slot], send_sem=q_send,
                recv_sem=q_recv.at[slot // per_chunk], device_id=pre_base[back] + ctx_base[away],
                device_id_type=pl.DeviceIdType.LOGICAL,
            ).start()
    for copy in loads[2:]:
        copy.wait()
    n_steps = ctx_len // block_len

    def chunk_step(chunk, carry):
        mine = pl.ds(pl.multiple_of(chunk * per_chunk, per_chunk), per_chunk)
        pltpu.make_async_copy(q_in.at[mine], q_in.at[mine], q_recv.at[chunk]).wait()
        q = q_in[mine].reshape(chunk_rows, DH)

        def score_step(j, top):
            for piece in range(block_len // PIECE):
                span = pl.ds(pl.multiple_of(j * block_len + piece * PIECE, PIECE), PIECE)
                s = lax.dot_general(q, k_raw[span, :], (((1,), (1,)), ((), ())), preferred_element_type=jnp.float32)
                scores[:, span] = s
                for i in range(PIECE // LANES):
                    top = jnp.maximum(top, s[:, i * LANES:(i + 1) * LANES])
            return top

        top = lax.fori_loop(0, n_steps, score_step, jnp.full((chunk_rows, LANES), -jnp.inf, jnp.float32))
        top = jnp.max(top, axis=1, keepdims=True) * log_scale
        acc[...] = jnp.zeros(acc.shape, jnp.float32)

        def weight_step(j, carry):
            added = None
            for piece in range(block_len // PIECE):
                span = pl.ds(pl.multiple_of(j * block_len + piece * PIECE, PIECE), PIECE)
                p = jnp.exp2(scores[:, span] * log_scale - top).astype(jnp.bfloat16)
                more = jnp.dot(p, v_ones[span, :], preferred_element_type=jnp.float32)
                added = more if added is None else added + more
            acc[...] += added
            return carry

        lax.fori_loop(0, n_steps, weight_step, 0)
        denom = acc[:, DH:]
        lse = top + jnp.log2(denom)
        part[mine] = (acc[:, :DH] / denom).astype(jnp.bfloat16).reshape(per_chunk, MSG, DH)
        own_lanes = iota((LANES, LANES), 1) == lax.rem(pre, per_tile) * MSG + iota((LANES, LANES), 0) % MSG
        for h in range(chunk_rows // LANES):
            spread = jnp.where(own_lanes, lse[h * LANES:(h + 1) * LANES], 0.0)
            stat[pl.ds(pl.multiple_of(chunk * per_chunk + h * per_tile, per_tile), per_tile)] = jnp.sum(
                spread.reshape(per_tile, MSG, LANES), axis=1, keepdims=True
            )

        def send_parts(which):
            for slot in range(which * per_chunk, (which + 1) * per_chunk):
                step, off = slots[slot]
                if slot == 0:
                    pltpu.make_async_copy(part.at[0], part_in.at[0, pre], part_recv).start()
                    pltpu.make_async_copy(stat.at[0], stat_in.at[0, pre], stat_recv).start()
                    continue
                for src, dst, send_sem, recv_sem in (
                    (part, part_in, part_send, part_recv), (stat, stat_in, stat_send, stat_recv)
                ):
                    pltpu.make_async_remote_copy(
                        src_ref=src.at[slot], dst_ref=dst.at[off, pre], send_sem=send_sem, recv_sem=recv_sem,
                        device_id=pre_base[step] + ctx_base[off], device_id_type=pl.DeviceIdType.LOGICAL,
                    ).start()

        for which in range(N_CHUNKS):
            pl.when(chunk == which)(functools.partial(send_parts, which))
        return carry

    lax.fori_loop(0, N_CHUNKS, chunk_step, 0)

    targets = jnp.concatenate([target_col] * GROUP, axis=0)
    r = iota((GROUP * n_req, rows), 0)
    lane = iota((GROUP * n_req, rows), 1)
    pick = (targets == lane // GROUP) & (r // n_req == lane % GROUP)
    pltpu.make_async_copy(stat_in, stat_in, stat_recv).wait()
    lses = [
        jnp.concatenate([
            jnp.sum(stat_in[chunk, h * per_tile:(h + 1) * per_tile], axis=0) for h in range(rows // LANES)
        ], axis=1)
        for chunk in range(n_ctx)
    ]
    highest = functools.reduce(jnp.maximum, lses)
    shares = [jnp.exp2(lse - highest) for lse in lses]
    total = functools.reduce(jnp.add, shares)
    pltpu.make_async_copy(part_in, part_in, part_recv).wait()
    answer = None
    for chunk in range(n_ctx):
        weight = jnp.where(pick, shares[chunk] / total, 0.0)
        coarse = weight.astype(jnp.bfloat16)
        fine = (weight - coarse.astype(jnp.float32)).astype(jnp.bfloat16)
        arrived = part_in[chunk].reshape(rows, DH)
        for term in (coarse, fine):
            more = jnp.dot(term, arrived, preferred_element_type=jnp.float32)
            answer = more if answer is None else answer + more
    answer = answer.astype(jnp.bfloat16)
    for e in range(GROUP):
        out[:, e * DH:(e + 1) * DH] = answer[e * n_req:(e + 1) * n_req]

    def sent(ref, sem):
        pltpu.make_async_copy(ref.at[pl.ds(1, n_slots - 1)], ref.at[pl.ds(1, n_slots - 1)], sem).wait()

    sent(q_in, q_send)
    sent(part, part_send)
    sent(stat, stat_send)


def body(queries, prefix_ids, keys, values):
    n_pre = lax.axis_size("prefix")
    n_ctx = lax.axis_size("ctx")
    ctx_len = keys.shape[1]
    rows = n_pre * MSG
    n_slots = n_pre * n_ctx
    chunk_rows = n_slots * MSG // N_CHUNKS
    block_len = min(2048, ctx_len)
    f32, bf16 = jnp.float32, jnp.bfloat16
    vmem = pl.BlockSpec(memory_space=pltpu.VMEM)
    hbm = pl.BlockSpec(memory_space=pl.ANY)
    dma = pltpu.SemaphoreType.DMA
    return pl.pallas_call(
        functools.partial(kernel, n_pre, n_ctx, block_len),
        out_shape=jax.ShapeDtypeStruct(queries.shape, bf16),
        in_specs=[hbm, hbm, hbm, hbm],
        out_specs=vmem,
        scratch_shapes=[
            pltpu.VMEM(queries.shape, bf16),
            pltpu.VMEM((1, queries.shape[0]), jnp.int32),
            pltpu.VMEM((n_pre, MSG, DH), bf16),
            pltpu.VMEM((n_slots, MSG, DH), bf16),
            pltpu.VMEM((ctx_len, DH), bf16),
            pltpu.VMEM((ctx_len, 2 * DH), bf16),
            pltpu.VMEM((chunk_rows, ctx_len), f32),
            pltpu.VMEM((chunk_rows, 2 * DH), f32),
            pltpu.VMEM((n_slots, MSG, DH), bf16),
            pltpu.VMEM((n_slots, 1, LANES), f32),
            pltpu.VMEM((n_ctx, n_pre, MSG, DH), bf16),
            pltpu.VMEM((n_ctx, n_pre, 1, LANES), f32),
            dma((4,)), dma, dma((N_CHUNKS,)), dma, dma, dma, dma,
        ],
        compiler_params=pltpu.CompilerParams(
            collective_id=0, has_side_effects=True, vmem_limit_bytes=VMEM_LIMIT
        ),
        cost_estimate=pl.CostEstimate(
            flops=4 * n_ctx * rows * ctx_len * DH, bytes_accessed=4 * ctx_len * DH,
            transcendentals=n_ctx * rows * ctx_len,
        ),
    )(queries, prefix_ids.reshape(1, -1), keys, values)


def solution(mesh):
    in_specs = (
        P(("prefix", "ctx"), "kvh"),
        P(("prefix", "ctx"), None),
        P("prefix", "ctx", "kvh"),
        P("prefix", "ctx", "kvh"),
    )
    out_specs = P(("prefix", "ctx"), "kvh")
    return jax.shard_map(body, mesh=mesh, in_specs=in_specs, out_specs=out_specs, check_vma=False)
```

```python
import functools
import math

import jax
import jax.numpy as jnp
from jax import lax
from jax.experimental import pallas as pl
from jax.experimental.pallas import tpu as pltpu
from jax.sharding import PartitionSpec as P

DH = 128
SEND_CAP = 2
GROUP = 8
VMEM_LIMIT = 63 * 1024 * 1024
LANES = 128
PIECE = 512
N_CHUNKS = 4
MSG = SEND_CAP * GROUP


def iota(shape, dim):
    return lax.broadcasted_iota(jnp.int32, shape, dim)


def slot_targets(ids_ref):
    n_req = ids_ref.shape[1]
    lane_req = iota((n_req, LANES), 1) % n_req
    row_req = iota((n_req, LANES), 0)
    row = jnp.concatenate([ids_ref[...]] * (LANES // n_req), axis=1)
    col = jnp.sum(jnp.where(iota((n_req, LANES), 1) == row_req, row, 0), axis=1, keepdims=True)
    same = col == row
    rank_row = jnp.sum(jnp.where(same & (row_req < lane_req), 1, 0), axis=0, keepdims=True)
    first = iota((n_req, LANES), 1) < row_req
    rank_col = jnp.sum(jnp.where(same & first, 1, 0), axis=1, keepdims=True)
    return row * SEND_CAP + rank_row, col * SEND_CAP + rank_col


def prefix_order(n_pre):
    side = n_pre // 2
    fours = [[0, side, 1, -1]]
    rest = [[side + 1, side - 1, 2, -2]]
    for far in range(2, side // 2):
        rest.append([side + far, side - far, far + 1, -far - 1])
    rest[-1][-1] = side + side // 2
    order = [step % n_pre for four in fours + rest[1:] + rest[:1] for step in four]
    assert sorted(order) == list(range(n_pre))
    return order


def kernel(
    n_pre, n_ctx, block_len, queries_hbm, ids_hbm, keys, values, out,
    queries, ids, outgoing, q_in, k_raw, v_ones, scores, acc, part, stat, part_in, stat_in,
    plane_sem, load_sem, q_send, q_recv, part_send, part_recv, stat_send, stat_recv,
):
    n_req, features = queries.shape
    ctx_len = keys.shape[1]
    rows = n_pre * MSG
    chunk_rows = n_pre * n_ctx * MSG // N_CHUNKS
    per_tile = LANES // MSG
    pre = lax.axis_index("prefix")
    ctx = lax.axis_index("ctx")
    log_scale = DH ** (-0.5) * math.log2(math.e)

    kvh, n_kvh = lax.axis_index("kvh"), lax.axis_size("kvh")
    pre_at = [lax.rem(pre + step, n_pre) for step in range(n_pre)]
    pre_base = [to * (n_ctx * n_kvh) + kvh for to in pre_at]
    ctx_base = [lax.rem(ctx + off, n_ctx) * n_kvh for off in range(n_ctx)]

    order = prefix_order(n_pre)
    near = [(step, 0) for step in order]
    slots = near + [(step, off) for step in order for off in (1, n_ctx - 1, 2)]
    n_slots = len(slots)
    per_chunk = n_slots // N_CHUNKS

    loads = [
        pltpu.make_async_copy(ids_hbm, ids, load_sem.at[2]),
        pltpu.make_async_copy(queries_hbm, queries, load_sem.at[3]),
        pltpu.make_async_copy(keys.at[0], k_raw, load_sem.at[0]),
        pltpu.make_async_copy(values.at[0], v_ones.at[:, pl.ds(0, DH)], load_sem.at[1]),
    ]
    for copy in loads:
        copy.start()
    barrier = pltpu.get_barrier_semaphore()

    for off in range(1, n_ctx):
        pl.semaphore_signal(
            barrier, inc=1, device_id=pre_base[0] + ctx_base[off], device_id_type=pl.DeviceIdType.LOGICAL
        )
    for step in order[1:]:
        pl.semaphore_signal(
            barrier, inc=1, device_id=pre_base[step] + ctx_base[0], device_id_type=pl.DeviceIdType.LOGICAL
        )
    for copy in loads[:2]:
        copy.wait()

    target_row, target_col = slot_targets(ids)
    r = iota((rows, LANES), 0)
    lane = iota((rows, LANES), 1)
    place = (jnp.broadcast_to(target_row, (rows, LANES)) == r // GROUP) & (r % GROUP == lane // n_req)
    by_head = jnp.concatenate([queries[:, e * DH:(e + 1) * DH] for e in range(GROUP)], axis=0)
    outgoing[...] = jnp.dot(
        jnp.where(place, 1.0, 0.0).astype(jnp.bfloat16), by_head, preferred_element_type=jnp.float32
    ).astype(jnp.bfloat16).reshape(n_pre, MSG, DH)

    pl.semaphore_wait(barrier, n_pre - 1 + n_ctx - 1)
    for off in range(1, n_ctx):
        pl.semaphore_signal(
            plane_sem, inc=1, device_id=pre_base[0] + ctx_base[off], device_id_type=pl.DeviceIdType.LOGICAL
        )

    def send_queries(first, last):
        for slot in range(first, last):
            step, off = slots[slot]
            back, away = (n_pre - step) % n_pre, (n_ctx - off) % n_ctx
            pltpu.make_async_remote_copy(
                src_ref=outgoing.at[pre_at[back]], dst_ref=q_in.at[slot], send_sem=q_send,
                recv_sem=q_recv.at[slot // per_chunk], device_id=pre_base[back] + ctx_base[away],
                device_id_type=pl.DeviceIdType.LOGICAL,
            ).start()

    pltpu.make_async_copy(outgoing.at[pre], q_in.at[0], q_recv.at[0]).start()
    send_queries(1, n_pre)
    v_ones[:, DH:] = jnp.ones((ctx_len, DH), jnp.bfloat16)

    pl.semaphore_wait(plane_sem, n_ctx - 1)
    send_queries(n_pre, n_slots)
    for copy in loads[2:]:
        copy.wait()
    n_steps = ctx_len // block_len

    def chunk_step(chunk, carry):
        mine = pl.ds(pl.multiple_of(chunk * per_chunk, per_chunk), per_chunk)
        pltpu.make_async_copy(q_in.at[mine], q_in.at[mine], q_recv.at[chunk]).wait()
        q = q_in[mine].reshape(chunk_rows, DH)

        def score_step(j, top):
            for piece in range(block_len // PIECE):
                span = pl.ds(pl.multiple_of(j * block_len + piece * PIECE, PIECE), PIECE)
                s = lax.dot_general(q, k_raw[span, :], (((1,), (1,)), ((), ())), preferred_element_type=jnp.float32)
                scores[:, span] = s
                for i in range(PIECE // LANES):
                    top = jnp.maximum(top, s[:, i * LANES:(i + 1) * LANES])
            return top

        top = lax.fori_loop(0, n_steps, score_step, jnp.full((chunk_rows, LANES), -jnp.inf, jnp.float32))
        top = jnp.max(top, axis=1, keepdims=True) * log_scale
        acc[...] = jnp.zeros(acc.shape, jnp.float32)

        def weight_step(j, carry):
            added = None
            for piece in range(block_len // PIECE):
                span = pl.ds(pl.multiple_of(j * block_len + piece * PIECE, PIECE), PIECE)
                p = jnp.exp2(scores[:, span] * log_scale - top).astype(jnp.bfloat16)
                more = jnp.dot(p, v_ones[span, :], preferred_element_type=jnp.float32)
                added = more if added is None else added + more
            acc[...] += added
            return carry

        lax.fori_loop(0, n_steps, weight_step, 0)
        denom = acc[:, DH:]
        lse = top + jnp.log2(denom)
        part[mine] = (acc[:, :DH] / denom).astype(jnp.bfloat16).reshape(per_chunk, MSG, DH)
        own_lanes = iota((LANES, LANES), 1) == lax.rem(pre, per_tile) * MSG + iota((LANES, LANES), 0) % MSG
        for h in range(chunk_rows // LANES):
            spread = jnp.where(own_lanes, lse[h * LANES:(h + 1) * LANES], 0.0)
            stat[pl.ds(pl.multiple_of(chunk * per_chunk + h * per_tile, per_tile), per_tile)] = jnp.sum(
                spread.reshape(per_tile, MSG, LANES), axis=1, keepdims=True
            )

        def send_parts(which):
            for slot in range(which * per_chunk, (which + 1) * per_chunk):
                step, off = slots[slot]
                if slot == 0:
                    pltpu.make_async_copy(part.at[0], part_in.at[0, pre], part_recv).start()
                    pltpu.make_async_copy(stat.at[0], stat_in.at[0, pre], stat_recv).start()
                    continue
                for src, dst, send_sem, recv_sem in (
                    (part, part_in, part_send, part_recv), (stat, stat_in, stat_send, stat_recv)
                ):
                    pltpu.make_async_remote_copy(
                        src_ref=src.at[slot], dst_ref=dst.at[off, pre], send_sem=send_sem, recv_sem=recv_sem,
                        device_id=pre_base[step] + ctx_base[off], device_id_type=pl.DeviceIdType.LOGICAL,
                    ).start()

        for which in range(N_CHUNKS):
            pl.when(chunk == which)(functools.partial(send_parts, which))
        return carry

    lax.fori_loop(0, N_CHUNKS, chunk_step, 0)

    targets = jnp.concatenate([target_col] * GROUP, axis=0)
    r = iota((GROUP * n_req, rows), 0)
    lane = iota((GROUP * n_req, rows), 1)
    pick = (targets == lane // GROUP) & (r // n_req == lane % GROUP)
    pltpu.make_async_copy(stat_in, stat_in, stat_recv).wait()
    lses = [
        jnp.concatenate([
            jnp.sum(stat_in[chunk, h * per_tile:(h + 1) * per_tile], axis=0) for h in range(rows // LANES)
        ], axis=1)
        for chunk in range(n_ctx)
    ]
    highest = functools.reduce(jnp.maximum, lses)
    shares = [jnp.exp2(lse - highest) for lse in lses]
    total = functools.reduce(jnp.add, shares)
    pltpu.make_async_copy(part_in, part_in, part_recv).wait()
    answer = None
    for chunk in range(n_ctx):
        weight = jnp.where(pick, shares[chunk] / total, 0.0)
        coarse = weight.astype(jnp.bfloat16)
        fine = (weight - coarse.astype(jnp.float32)).astype(jnp.bfloat16)
        arrived = part_in[chunk].reshape(rows, DH)
        for term in (coarse, fine):
            more = jnp.dot(term, arrived, preferred_element_type=jnp.float32)
            answer = more if answer is None else answer + more
    answer = answer.astype(jnp.bfloat16)
    for e in range(GROUP):
        out[:, e * DH:(e + 1) * DH] = answer[e * n_req:(e + 1) * n_req]

    def sent(ref, sem):
        pltpu.make_async_copy(ref.at[pl.ds(1, n_slots - 1)], ref.at[pl.ds(1, n_slots - 1)], sem).wait()

    sent(q_in, q_send)
    sent(part, part_send)
    sent(stat, stat_send)


def body(queries, prefix_ids, keys, values):
    n_pre = lax.axis_size("prefix")
    n_ctx = lax.axis_size("ctx")
    ctx_len = keys.shape[1]
    rows = n_pre * MSG
    n_slots = n_pre * n_ctx
    chunk_rows = n_slots * MSG // N_CHUNKS
    block_len = min(2048, ctx_len)
    f32, bf16 = jnp.float32, jnp.bfloat16
    vmem = pl.BlockSpec(memory_space=pltpu.VMEM)
    hbm = pl.BlockSpec(memory_space=pl.ANY)
    dma = pltpu.SemaphoreType.DMA
    return pl.pallas_call(
        functools.partial(kernel, n_pre, n_ctx, block_len),
        out_shape=jax.ShapeDtypeStruct(queries.shape, bf16),
        in_specs=[hbm, hbm, hbm, hbm],
        out_specs=vmem,
        scratch_shapes=[
            pltpu.VMEM(queries.shape, bf16),
            pltpu.VMEM((1, queries.shape[0]), jnp.int32),
            pltpu.VMEM((n_pre, MSG, DH), bf16),
            pltpu.VMEM((n_slots, MSG, DH), bf16),
            pltpu.VMEM((ctx_len, DH), bf16),
            pltpu.VMEM((ctx_len, 2 * DH), bf16),
            pltpu.VMEM((chunk_rows, ctx_len), f32),
            pltpu.VMEM((chunk_rows, 2 * DH), f32),
            pltpu.VMEM((n_slots, MSG, DH), bf16),
            pltpu.VMEM((n_slots, 1, LANES), f32),
            pltpu.VMEM((n_ctx, n_pre, MSG, DH), bf16),
            pltpu.VMEM((n_ctx, n_pre, 1, LANES), f32),
            pltpu.SemaphoreType.REGULAR, dma((4,)), dma, dma((N_CHUNKS,)), dma, dma, dma, dma,
        ],
        compiler_params=pltpu.CompilerParams(
            collective_id=0, has_side_effects=True, vmem_limit_bytes=VMEM_LIMIT
        ),
        cost_estimate=pl.CostEstimate(
            flops=4 * n_ctx * rows * ctx_len * DH, bytes_accessed=4 * ctx_len * DH,
            transcendentals=n_ctx * rows * ctx_len,
        ),
    )(queries, prefix_ids.reshape(1, -1), keys, values)


def solution(mesh):
    in_specs = (
        P(("prefix", "ctx"), "kvh"),
        P(("prefix", "ctx"), None),
        P("prefix", "ctx", "kvh"),
        P("prefix", "ctx", "kvh"),
    )
    out_specs = P(("prefix", "ctx"), "kvh")
    return jax.shard_map(body, mesh=mesh, in_specs=in_specs, out_specs=out_specs, check_vma=False)
```

```python
import functools
import math

import jax
import jax.numpy as jnp
from jax import lax
from jax.experimental import pallas as pl
from jax.experimental.pallas import tpu as pltpu
from jax.sharding import PartitionSpec as P

DH = 128
SEND_CAP = 2
GROUP = 8
VMEM_LIMIT = 63 * 1024 * 1024
LANES = 128
PIECE = 512
MSG = SEND_CAP * GROUP


def iota(shape, dim):
    return lax.broadcasted_iota(jnp.int32, shape, dim)


def slot_targets(ids_ref):
    n_req = ids_ref.shape[1]
    lane_req = iota((n_req, LANES), 1) % n_req
    row_req = iota((n_req, LANES), 0)
    row = jnp.concatenate([ids_ref[...]] * (LANES // n_req), axis=1)
    col = jnp.sum(jnp.where(iota((n_req, LANES), 1) == row_req, row, 0), axis=1, keepdims=True)
    same = col == row
    rank_row = jnp.sum(jnp.where(same & (row_req < lane_req), 1, 0), axis=0, keepdims=True)
    first = iota((n_req, LANES), 1) < row_req
    rank_col = jnp.sum(jnp.where(same & first, 1, 0), axis=1, keepdims=True)
    return row * SEND_CAP + rank_row, col * SEND_CAP + rank_col


def kernel(
    n_pre, n_ctx, block_len, queries_hbm, ids_hbm, keys, values, out,
    queries, ids, outgoing, q_in, k_raw, v_ones, scores, acc, part, stat, part_in, stat_in,
    ready_low, ready_high, load_sem, q_send, q_recv, part_send, part_recv, stat_send, stat_recv,
):
    n_req, features = queries.shape
    ctx_len = keys.shape[1]
    rows = n_pre * MSG
    per_tile = LANES // MSG
    pre = lax.axis_index("prefix")
    ctx = lax.axis_index("ctx")
    log_scale = DH ** (-0.5) * math.log2(math.e)

    kvh, n_kvh = lax.axis_index("kvh"), lax.axis_size("kvh")
    pre_at = [lax.rem(pre + step, n_pre) for step in range(n_pre)]
    pre_base = [to * (n_ctx * n_kvh) + kvh for to in pre_at]
    rank = ctx * n_pre + pre
    half_len = n_pre // 2
    ready = (ready_low, ready_high)

    def in_half(index, half):
        return index >= half_len if half else index < half_len

    def device(step, to_ctx):
        return pre_base[step % n_pre] + to_ctx * n_kvh

    def later_ones(to_ctx, act):
        @pl.when(to_ctx > ctx)
        def _():
            for step in range(1, n_pre + 1):
                act(step)

        @pl.when(to_ctx == ctx)
        def _():
            for step in range(1, n_pre):
                pl.when(pre + step < n_pre)(functools.partial(act, step))

    def earlier_ones(to_ctx, act):
        @pl.when(to_ctx < ctx)
        def _():
            for step in range(1, n_pre + 1):
                act(n_pre - step)

        @pl.when(to_ctx == ctx)
        def _():
            for step in range(1, n_pre):
                pl.when(pre >= step)(functools.partial(act, n_pre - step))

    def over_planes(first, last, loop, act):
        def plane(to_ctx, carry):
            loop(to_ctx, functools.partial(act, to_ctx))
            return carry

        lax.fori_loop(first, last, plane, 0)

    def send_query(to_ctx, step):
        pltpu.make_async_remote_copy(
            src_ref=outgoing.at[pre_at[step % n_pre]], dst_ref=q_in.at[ctx, pre], send_sem=q_send, recv_sem=q_recv.at[ctx],
            device_id=device(step, to_ctx), device_id_type=pl.DeviceIdType.LOGICAL,
        ).start()

    loads = [
        pltpu.make_async_copy(ids_hbm, ids, load_sem.at[2]),
        pltpu.make_async_copy(queries_hbm, queries, load_sem.at[3]),
        pltpu.make_async_copy(keys.at[0], k_raw, load_sem.at[0]),
        pltpu.make_async_copy(values.at[0], v_ones.at[:, pl.ds(0, DH)], load_sem.at[1]),
    ]
    for copy in loads:
        copy.start()
    barrier = pltpu.get_barrier_semaphore()

    over_planes(ctx, n_ctx, later_ones, lambda to_ctx, step: pl.semaphore_signal(
        barrier, inc=1, device_id=device(step, to_ctx), device_id_type=pl.DeviceIdType.LOGICAL
    ))

    @pl.when(rank > 0)
    def _():
        pl.semaphore_wait(barrier, rank)

    for half in range(2):
        @pl.when(in_half(pre, half))
        def _():
            over_planes(0, ctx + 1, earlier_ones, lambda to_ctx, step: pl.semaphore_signal(
                ready[half].at[ctx], inc=1, device_id=device(step, to_ctx), device_id_type=pl.DeviceIdType.LOGICAL
            ))

    for copy in loads[:2]:
        copy.wait()

    target_row, target_col = slot_targets(ids)
    r = iota((rows, LANES), 0)
    lane = iota((rows, LANES), 1)
    place = (jnp.broadcast_to(target_row, (rows, LANES)) == r // GROUP) & (r % GROUP == lane // n_req)
    by_head = jnp.concatenate([queries[:, e * DH:(e + 1) * DH] for e in range(GROUP)], axis=0)
    outgoing[...] = jnp.dot(
        jnp.where(place, 1.0, 0.0).astype(jnp.bfloat16), by_head, preferred_element_type=jnp.float32
    ).astype(jnp.bfloat16).reshape(n_pre, MSG, DH)

    pltpu.make_async_copy(outgoing.at[pre], q_in.at[ctx, pre], q_recv.at[ctx]).start()
    over_planes(0, ctx + 1, earlier_ones, send_query)
    v_ones[:, DH:] = jnp.ones((ctx_len, DH), jnp.bfloat16)

    def serve(to_ctx, carry):
        for half in range(2):
            whole = to_ctx > ctx
            if half:
                whole = whole | ((to_ctx == ctx) & in_half(pre, 0))
            later = (half + 1) * half_len - 1 - pre

            @pl.when(whole)
            def _():
                pl.semaphore_wait(ready[half].at[to_ctx], half_len)
                for step in range(1, n_pre + 1):
                    pl.when(in_half(pre_at[step % n_pre], half))(functools.partial(send_query, to_ctx, step))

            @pl.when((to_ctx == ctx) & in_half(pre, half) & (later > 0))
            def _():
                pl.semaphore_wait(ready[half].at[to_ctx], later)
                for step in range(1, half_len):
                    pl.when(pre + step < (half + 1) * half_len)(functools.partial(send_query, to_ctx, step))

        return carry

    lax.fori_loop(0, n_ctx, serve, 0)
    for copy in loads[2:]:
        copy.wait()
    own_lanes = iota((LANES, LANES), 1) == lax.rem(pre, per_tile) * MSG + iota((LANES, LANES), 0) % MSG
    n_steps = ctx_len // block_len

    def chunk_step(chunk, carry):
        pltpu.make_async_copy(q_in.at[chunk], q_in.at[chunk], q_recv.at[chunk]).wait()
        q = q_in[chunk].reshape(rows, DH)

        def score_step(j, top):
            for piece in range(block_len // PIECE):
                span = pl.ds(pl.multiple_of(j * block_len + piece * PIECE, PIECE), PIECE)
                s = lax.dot_general(q, k_raw[span, :], (((1,), (1,)), ((), ())), preferred_element_type=jnp.float32)
                scores[:, span] = s
                for i in range(PIECE // LANES):
                    top = jnp.maximum(top, s[:, i * LANES:(i + 1) * LANES])
            return top

        top = lax.fori_loop(0, n_steps, score_step, jnp.full((rows, LANES), -jnp.inf, jnp.float32))
        top = jnp.max(top, axis=1, keepdims=True) * log_scale
        acc[...] = jnp.zeros(acc.shape, jnp.float32)

        def weight_step(j, carry):
            added = None
            for piece in range(block_len // PIECE):
                span = pl.ds(pl.multiple_of(j * block_len + piece * PIECE, PIECE), PIECE)
                p = jnp.exp2(scores[:, span] * log_scale - top).astype(jnp.bfloat16)
                more = jnp.dot(p, v_ones[span, :], preferred_element_type=jnp.float32)
                added = more if added is None else added + more
            acc[...] += added
            return carry

        lax.fori_loop(0, n_steps, weight_step, 0)
        denom = acc[:, DH:]
        lse = top + jnp.log2(denom)
        part[chunk] = (acc[:, :DH] / denom).astype(jnp.bfloat16).reshape(n_pre, MSG, DH)
        for h in range(rows // LANES):
            spread = jnp.where(own_lanes, lse[h * LANES:(h + 1) * LANES], 0.0)
            stat[chunk, h * per_tile:(h + 1) * per_tile] = jnp.sum(
                spread.reshape(per_tile, MSG, LANES), axis=1, keepdims=True
            )

        def send_part(step):
            to = pre_at[step]
            for src, dst, send_sem, recv_sem in (
                (part, part_in, part_send, part_recv), (stat, stat_in, stat_send, stat_recv)
            ):
                pltpu.make_async_remote_copy(
                    src_ref=src.at[chunk, to], dst_ref=dst.at[ctx, pre], send_sem=send_sem, recv_sem=recv_sem,
                    device_id=device(step, chunk), device_id_type=pl.DeviceIdType.LOGICAL,
                ).start()

        @pl.when(chunk == ctx)
        def _():
            pltpu.make_async_copy(part.at[chunk, pre], part_in.at[ctx, pre], part_recv).start()
            pltpu.make_async_copy(stat.at[chunk, pre], stat_in.at[ctx, pre], stat_recv).start()

        @pl.when(chunk != ctx)
        def _():
            send_part(0)

        for step in range(1, n_pre):
            send_part(step)
        return carry

    lax.fori_loop(0, n_ctx, chunk_step, 0)

    targets = jnp.concatenate([target_col] * GROUP, axis=0)
    r = iota((GROUP * n_req, rows), 0)
    lane = iota((GROUP * n_req, rows), 1)
    pick = (targets == lane // GROUP) & (r // n_req == lane % GROUP)
    pltpu.make_async_copy(stat_in, stat_in, stat_recv).wait()
    lses = [
        jnp.concatenate([
            jnp.sum(stat_in[chunk, h * per_tile:(h + 1) * per_tile], axis=0) for h in range(rows // LANES)
        ], axis=1)
        for chunk in range(n_ctx)
    ]
    highest = functools.reduce(jnp.maximum, lses)
    shares = [jnp.exp2(lse - highest) for lse in lses]
    total = functools.reduce(jnp.add, shares)
    pltpu.make_async_copy(part_in, part_in, part_recv).wait()
    answer = None
    for chunk in range(n_ctx):
        weight = jnp.where(pick, shares[chunk] / total, 0.0)
        coarse = weight.astype(jnp.bfloat16)
        fine = (weight - coarse.astype(jnp.float32)).astype(jnp.bfloat16)
        arrived = part_in[chunk].reshape(rows, DH)
        for term in (coarse, fine):
            more = jnp.dot(term, arrived, preferred_element_type=jnp.float32)
            answer = more if answer is None else answer + more
    answer = answer.astype(jnp.bfloat16)
    for e in range(GROUP):
        out[:, e * DH:(e + 1) * DH] = answer[e * n_req:(e + 1) * n_req]

    def sent(ref, sem):
        pltpu.make_async_copy(ref.at[pl.ds(1, n_ctx - 1)], ref.at[pl.ds(1, n_ctx - 1)], sem).wait()
        pltpu.make_async_copy(ref.at[0, pl.ds(1, n_pre - 1)], ref.at[0, pl.ds(1, n_pre - 1)], sem).wait()

    sent(q_in, q_send)
    sent(part, part_send)
    sent(stat, stat_send)


def body(queries, prefix_ids, keys, values):
    n_pre = lax.axis_size("prefix")
    n_ctx = lax.axis_size("ctx")
    ctx_len = keys.shape[1]
    rows = n_pre * MSG
    block_len = min(2048, ctx_len)
    f32, bf16 = jnp.float32, jnp.bfloat16
    vmem = pl.BlockSpec(memory_space=pltpu.VMEM)
    hbm = pl.BlockSpec(memory_space=pl.ANY)
    dma = pltpu.SemaphoreType.DMA
    return pl.pallas_call(
        functools.partial(kernel, n_pre, n_ctx, block_len),
        out_shape=jax.ShapeDtypeStruct(queries.shape, bf16),
        in_specs=[hbm, hbm, hbm, hbm],
        out_specs=vmem,
        scratch_shapes=[
            pltpu.VMEM(queries.shape, bf16),
            pltpu.VMEM((1, queries.shape[0]), jnp.int32),
            pltpu.VMEM((n_pre, MSG, DH), bf16),
            pltpu.VMEM((n_ctx, n_pre, MSG, DH), bf16),
            pltpu.VMEM((ctx_len, DH), bf16),
            pltpu.VMEM((ctx_len, 2 * DH), bf16),
            pltpu.VMEM((rows, ctx_len), f32),
            pltpu.VMEM((rows, 2 * DH), f32),
            pltpu.VMEM((n_ctx, n_pre, MSG, DH), bf16),
            pltpu.VMEM((n_ctx, n_pre, 1, LANES), f32),
            pltpu.VMEM((n_ctx, n_pre, MSG, DH), bf16),
            pltpu.VMEM((n_ctx, n_pre, 1, LANES), f32),
            pltpu.SemaphoreType.REGULAR((n_ctx,)), pltpu.SemaphoreType.REGULAR((n_ctx,)), dma((4,)), dma, dma((n_ctx,)), dma, dma, dma, dma,
        ],
        compiler_params=pltpu.CompilerParams(
            collective_id=0, has_side_effects=True, vmem_limit_bytes=VMEM_LIMIT
        ),
        cost_estimate=pl.CostEstimate(
            flops=4 * n_ctx * rows * ctx_len * DH, bytes_accessed=4 * ctx_len * DH,
            transcendentals=n_ctx * rows * ctx_len,
        ),
    )(queries, prefix_ids.reshape(1, -1), keys, values)


def solution(mesh):
    in_specs = (
        P(("prefix", "ctx"), "kvh"),
        P(("prefix", "ctx"), None),
        P("prefix", "ctx", "kvh"),
        P("prefix", "ctx", "kvh"),
    )
    out_specs = P(("prefix", "ctx"), "kvh")
    return jax.shard_map(body, mesh=mesh, in_specs=in_specs, out_specs=out_specs, check_vma=False)
```

```python
import functools
import math

import jax
import jax.numpy as jnp
from jax import lax
from jax.experimental import pallas as pl
from jax.experimental.pallas import tpu as pltpu
from jax.sharding import PartitionSpec as P

DH = 128
SEND_CAP = 2
GROUP = 8
VMEM_LIMIT = 63 * 1024 * 1024
LANES = 128
PIECE = 512
MSG = SEND_CAP * GROUP


def iota(shape, dim):
    return lax.broadcasted_iota(jnp.int32, shape, dim)


def slot_targets(ids_ref):
    n_req = ids_ref.shape[1]
    lane_req = iota((n_req, LANES), 1) % n_req
    row_req = iota((n_req, LANES), 0)
    row = jnp.concatenate([ids_ref[...]] * (LANES // n_req), axis=1)
    col = jnp.sum(jnp.where(iota((n_req, LANES), 1) == row_req, row, 0), axis=1, keepdims=True)
    same = col == row
    rank_row = jnp.sum(jnp.where(same & (row_req < lane_req), 1, 0), axis=0, keepdims=True)
    first = iota((n_req, LANES), 1) < row_req
    rank_col = jnp.sum(jnp.where(same & first, 1, 0), axis=1, keepdims=True)
    return row * SEND_CAP + rank_row, col * SEND_CAP + rank_col


def kernel(
    n_pre, n_ctx, block_len, queries_hbm, ids_hbm, keys, values, out,
    queries, ids, outgoing, q_in, k_raw, v_ones, scores, acc, part, stat, part_in, stat_in,
    ready_low, ready_high, load_sem, q_send, q_recv, part_send, part_recv, stat_send, stat_recv,
):
    n_req, features = queries.shape
    ctx_len = keys.shape[1]
    rows = n_pre * MSG
    per_tile = LANES // MSG
    pre = lax.axis_index("prefix")
    ctx = lax.axis_index("ctx")
    log_scale = DH ** (-0.5) * math.log2(math.e)

    kvh, n_kvh = lax.axis_index("kvh"), lax.axis_size("kvh")
    pre_at = [lax.rem(pre + step, n_pre) for step in range(n_pre)]
    pre_base = [to * (n_ctx * n_kvh) + kvh for to in pre_at]
    rank = ctx * n_pre + pre
    half_len = n_pre // 2
    ready = (ready_low, ready_high)

    def in_half(index, half):
        return index >= half_len if half else index < half_len

    def device(step, to_ctx):
        return pre_base[step % n_pre] + to_ctx * n_kvh

    def later_ones(to_ctx, act):
        @pl.when(to_ctx > ctx)
        def _():
            for step in range(1, n_pre + 1):
                act(step)

        @pl.when(to_ctx == ctx)
        def _():
            for step in range(1, n_pre):
                pl.when(pre + step < n_pre)(functools.partial(act, step))

    def earlier_ones(to_ctx, act):
        @pl.when(to_ctx < ctx)
        def _():
            for step in range(1, n_pre + 1):
                act(n_pre - step)

        @pl.when(to_ctx == ctx)
        def _():
            for step in range(1, n_pre):
                pl.when(pre >= step)(functools.partial(act, n_pre - step))

    def over_planes(first, last, loop, act):
        def plane(to_ctx, carry):
            loop(to_ctx, functools.partial(act, to_ctx))
            return carry

        lax.fori_loop(first, last, plane, 0)

    def send_query(to_ctx, step):
        pltpu.make_async_remote_copy(
            src_ref=outgoing.at[pre_at[step % n_pre]], dst_ref=q_in.at[ctx, pre], send_sem=q_send, recv_sem=q_recv.at[ctx],
            device_id=device(step, to_ctx), device_id_type=pl.DeviceIdType.LOGICAL,
        ).start()

    loads = [
        pltpu.make_async_copy(ids_hbm, ids, load_sem.at[2]),
        pltpu.make_async_copy(queries_hbm, queries, load_sem.at[3]),
        pltpu.make_async_copy(keys.at[0], k_raw, load_sem.at[0]),
        pltpu.make_async_copy(values.at[0], v_ones.at[:, pl.ds(0, DH)], load_sem.at[1]),
    ]
    for copy in loads:
        copy.start()
    barrier = pltpu.get_barrier_semaphore()

    over_planes(ctx, n_ctx, later_ones, lambda to_ctx, step: pl.semaphore_signal(
        barrier, inc=1, device_id=device(step, to_ctx), device_id_type=pl.DeviceIdType.LOGICAL
    ))

    @pl.when(rank > 0)
    def _():
        pl.semaphore_wait(barrier, rank)

    for half in range(2):
        @pl.when(in_half(pre, half))
        def _():
            over_planes(0, ctx + 1, earlier_ones, lambda to_ctx, step: pl.semaphore_signal(
                ready[half].at[ctx], inc=1, device_id=device(step, to_ctx), device_id_type=pl.DeviceIdType.LOGICAL
            ))

    for copy in loads[:2]:
        copy.wait()

    target_row, target_col = slot_targets(ids)
    r = iota((rows, LANES), 0)
    lane = iota((rows, LANES), 1)
    place = (jnp.broadcast_to(target_row, (rows, LANES)) == r // GROUP) & (r % GROUP == lane // n_req)
    by_head = jnp.concatenate([queries[:, e * DH:(e + 1) * DH] for e in range(GROUP)], axis=0)
    outgoing[...] = jnp.dot(
        jnp.where(place, 1.0, 0.0).astype(jnp.bfloat16), by_head, preferred_element_type=jnp.float32
    ).astype(jnp.bfloat16).reshape(n_pre, MSG, DH)

    pltpu.make_async_copy(outgoing.at[pre], q_in.at[ctx, pre], q_recv.at[ctx]).start()
    over_planes(0, ctx + 1, earlier_ones, send_query)
    v_ones[:, DH:] = jnp.ones((ctx_len, DH), jnp.bfloat16)

    def serve(to_ctx, carry):
        for half in range(2):
            whole = to_ctx > ctx
            if half:
                whole = whole | ((to_ctx == ctx) & in_half(pre, 0))
            later = (half + 1) * half_len - 1 - pre

            @pl.when(whole)
            def _():
                pl.semaphore_wait(ready[half].at[to_ctx], half_len)
                for step in range(1, n_pre + 1):
                    pl.when(in_half(pre_at[step % n_pre], half))(functools.partial(send_query, to_ctx, step))

            @pl.when((to_ctx == ctx) & in_half(pre, half) & (later > 0))
            def _():
                pl.semaphore_wait(ready[half].at[to_ctx], later)
                for step in range(1, half_len):
                    pl.when(pre + step < (half + 1) * half_len)(functools.partial(send_query, to_ctx, step))

        return carry

    lax.fori_loop(0, n_ctx, serve, 0)
    for copy in loads[2:]:
        copy.wait()
    own_lanes = iota((LANES, LANES), 1) == lax.rem(pre, per_tile) * MSG + iota((LANES, LANES), 0) % MSG
    n_steps = ctx_len // block_len

    def chunk_step(chunk, carry):
        pltpu.make_async_copy(q_in.at[chunk], q_in.at[chunk], q_recv.at[chunk]).wait()
        q = q_in[chunk].reshape(rows, DH)

        def score_step(j, top):
            for piece in range(block_len // PIECE):
                span = pl.ds(pl.multiple_of(j * block_len + piece * PIECE, PIECE), PIECE)
                s = lax.dot_general(q, k_raw[span, :], (((1,), (1,)), ((), ())), preferred_element_type=jnp.float32)
                scores[:, span] = s
                for i in range(PIECE // LANES):
                    top = jnp.maximum(top, s[:, i * LANES:(i + 1) * LANES])
            return top

        top = lax.fori_loop(0, n_steps, score_step, jnp.full((rows, LANES), -jnp.inf, jnp.float32))
        top = jnp.max(top, axis=1, keepdims=True) * log_scale
        acc[...] = jnp.zeros(acc.shape, jnp.float32)

        def weight_step(j, carry):
            added = None
            for piece in range(block_len // PIECE):
                span = pl.ds(pl.multiple_of(j * block_len + piece * PIECE, PIECE), PIECE)
                p = jnp.exp2(scores[:, span] * log_scale - top).astype(jnp.bfloat16)
                more = jnp.dot(p, v_ones[span, :], preferred_element_type=jnp.float32)
                added = more if added is None else added + more
            acc[...] += added
            return carry

        lax.fori_loop(0, n_steps, weight_step, 0)
        denom = acc[:, DH:]
        lse = top + jnp.log2(denom)
        part[chunk] = (acc[:, :DH] / denom).astype(jnp.bfloat16).reshape(n_pre, MSG, DH)
        for h in range(rows // LANES):
            spread = jnp.where(own_lanes, lse[h * LANES:(h + 1) * LANES], 0.0)
            stat[chunk, h * per_tile:(h + 1) * per_tile] = jnp.sum(
                spread.reshape(per_tile, MSG, LANES), axis=1, keepdims=True
            )

        def send_part(step):
            to = pre_at[step]
            for src, dst, send_sem, recv_sem in (
                (part, part_in, part_send, part_recv), (stat, stat_in, stat_send, stat_recv)
            ):
                pltpu.make_async_remote_copy(
                    src_ref=src.at[chunk, to], dst_ref=dst.at[ctx, pre], send_sem=send_sem, recv_sem=recv_sem,
                    device_id=device(step, chunk), device_id_type=pl.DeviceIdType.LOGICAL,
                ).start()

        @pl.when(chunk == ctx)
        def _():
            pltpu.make_async_copy(part.at[chunk, pre], part_in.at[ctx, pre], part_recv).start()
            pltpu.make_async_copy(stat.at[chunk, pre], stat_in.at[ctx, pre], stat_recv).start()

        @pl.when(chunk != ctx)
        def _():
            send_part(0)

        for step in range(1, n_pre):
            send_part(step)
        return carry

    lax.fori_loop(0, n_ctx, chunk_step, 0)

    targets = jnp.concatenate([target_col] * GROUP, axis=0)
    r = iota((GROUP * n_req, rows), 0)
    lane = iota((GROUP * n_req, rows), 1)
    pick = (targets == lane // GROUP) & (r // n_req == lane % GROUP)
    pltpu.make_async_copy(stat_in, stat_in, stat_recv).wait()
    lses = [
        jnp.concatenate([
            jnp.sum(stat_in[chunk, h * per_tile:(h + 1) * per_tile], axis=0) for h in range(rows // LANES)
        ], axis=1)
        for chunk in range(n_ctx)
    ]
    highest = functools.reduce(jnp.maximum, lses)
    shares = [jnp.exp2(lse - highest) for lse in lses]
    total = functools.reduce(jnp.add, shares)
    pltpu.make_async_copy(part_in, part_in, part_recv).wait()
    answer = None
    for chunk in range(n_ctx):
        weight = jnp.where(pick, shares[chunk] / total, 0.0)
        coarse = weight.astype(jnp.bfloat16)
        fine = (weight - coarse.astype(jnp.float32)).astype(jnp.bfloat16)
        arrived = part_in[chunk].reshape(rows, DH)
        for term in (coarse, fine):
            more = jnp.dot(term, arrived, preferred_element_type=jnp.float32)
            answer = more if answer is None else answer + more
    answer = answer.astype(jnp.bfloat16)
    for e in range(GROUP):
        out[:, e * DH:(e + 1) * DH] = answer[e * n_req:(e + 1) * n_req]

    def sent(ref, sem):
        pltpu.make_async_copy(ref.at[pl.ds(1, n_ctx - 1)], ref.at[pl.ds(1, n_ctx - 1)], sem).wait()
        pltpu.make_async_copy(ref.at[0, pl.ds(1, n_pre - 1)], ref.at[0, pl.ds(1, n_pre - 1)], sem).wait()

    sent(q_in, q_send)
    sent(part, part_send)
    sent(stat, stat_send)


def body(queries, prefix_ids, keys, values):
    n_pre = lax.axis_size("prefix")
    n_ctx = lax.axis_size("ctx")
    ctx_len = keys.shape[1]
    rows = n_pre * MSG
    block_len = min(1024, ctx_len)
    f32, bf16 = jnp.float32, jnp.bfloat16
    vmem = pl.BlockSpec(memory_space=pltpu.VMEM)
    hbm = pl.BlockSpec(memory_space=pl.ANY)
    dma = pltpu.SemaphoreType.DMA
    return pl.pallas_call(
        functools.partial(kernel, n_pre, n_ctx, block_len),
        out_shape=jax.ShapeDtypeStruct(queries.shape, bf16),
        in_specs=[hbm, hbm, hbm, hbm],
        out_specs=vmem,
        scratch_shapes=[
            pltpu.VMEM(queries.shape, bf16),
            pltpu.VMEM((1, queries.shape[0]), jnp.int32),
            pltpu.VMEM((n_pre, MSG, DH), bf16),
            pltpu.VMEM((n_ctx, n_pre, MSG, DH), bf16),
            pltpu.VMEM((ctx_len, DH), bf16),
            pltpu.VMEM((ctx_len, 2 * DH), bf16),
            pltpu.VMEM((rows, ctx_len), f32),
            pltpu.VMEM((rows, 2 * DH), f32),
            pltpu.VMEM((n_ctx, n_pre, MSG, DH), bf16),
            pltpu.VMEM((n_ctx, n_pre, 1, LANES), f32),
            pltpu.VMEM((n_ctx, n_pre, MSG, DH), bf16),
            pltpu.VMEM((n_ctx, n_pre, 1, LANES), f32),
            pltpu.SemaphoreType.REGULAR((n_ctx,)), pltpu.SemaphoreType.REGULAR((n_ctx,)), dma((4,)), dma, dma((n_ctx,)), dma, dma, dma, dma,
        ],
        compiler_params=pltpu.CompilerParams(
            collective_id=0, has_side_effects=True, vmem_limit_bytes=VMEM_LIMIT
        ),
        cost_estimate=pl.CostEstimate(
            flops=4 * n_ctx * rows * ctx_len * DH, bytes_accessed=4 * ctx_len * DH,
            transcendentals=n_ctx * rows * ctx_len,
        ),
    )(queries, prefix_ids.reshape(1, -1), keys, values)


def solution(mesh):
    in_specs = (
        P(("prefix", "ctx"), "kvh"),
        P(("prefix", "ctx"), None),
        P("prefix", "ctx", "kvh"),
        P("prefix", "ctx", "kvh"),
    )
    out_specs = P(("prefix", "ctx"), "kvh")
    return jax.shard_map(body, mesh=mesh, in_specs=in_specs, out_specs=out_specs, check_vma=False)
```

```python
import functools
import math

import jax
import jax.numpy as jnp
from jax import lax
from jax.experimental import pallas as pl
from jax.experimental.pallas import tpu as pltpu
from jax.sharding import PartitionSpec as P

DH = 128
SEND_CAP = 2
GROUP = 8
VMEM_LIMIT = 63 * 1024 * 1024
LANES = 128
PIECE = 512
MSG = SEND_CAP * GROUP


def iota(shape, dim):
    return lax.broadcasted_iota(jnp.int32, shape, dim)


def slot_targets(ids_ref):
    n_req = ids_ref.shape[1]
    lane_req = iota((n_req, LANES), 1) % n_req
    row_req = iota((n_req, LANES), 0)
    row = jnp.concatenate([ids_ref[...]] * (LANES // n_req), axis=1)
    col = jnp.sum(jnp.where(iota((n_req, LANES), 1) == row_req, row, 0), axis=1, keepdims=True)
    same = col == row
    rank_row = jnp.sum(jnp.where(same & (row_req < lane_req), 1, 0), axis=0, keepdims=True)
    first = iota((n_req, LANES), 1) < row_req
    rank_col = jnp.sum(jnp.where(same & first, 1, 0), axis=1, keepdims=True)
    return row * SEND_CAP + rank_row, col * SEND_CAP + rank_col


def kernel(
    n_pre, n_ctx, block_len, queries_hbm, ids_hbm, keys, values, out,
    queries, ids, outgoing, q_in, k_raw, v_ones, scores, acc, part, stat, part_in, stat_in,
    ready_low, ready_high, load_sem, q_send, q_recv, part_send, part_recv, stat_send, stat_recv,
):
    n_req, features = queries.shape
    ctx_len = keys.shape[1]
    rows = n_pre * MSG
    per_tile = LANES // MSG
    pre = lax.axis_index("prefix")
    ctx = lax.axis_index("ctx")
    log_scale = DH ** (-0.5) * math.log2(math.e)

    kvh, n_kvh = lax.axis_index("kvh"), lax.axis_size("kvh")
    pre_at = [lax.rem(pre + step, n_pre) for step in range(n_pre)]
    pre_base = [to * (n_ctx * n_kvh) + kvh for to in pre_at]
    rank = ctx * n_pre + pre
    half_len = n_pre // 2
    ready = (ready_low, ready_high)

    def in_half(index, half):
        return index >= half_len if half else index < half_len

    def device(step, to_ctx):
        return pre_base[step % n_pre] + to_ctx * n_kvh

    def later_ones(to_ctx, act):
        @pl.when(to_ctx > ctx)
        def _():
            for step in range(1, n_pre + 1):
                act(step)

        @pl.when(to_ctx == ctx)
        def _():
            for step in range(1, n_pre):
                pl.when(pre + step < n_pre)(functools.partial(act, step))

    def earlier_ones(to_ctx, act):
        @pl.when(to_ctx < ctx)
        def _():
            for step in range(1, n_pre + 1):
                act(n_pre - step)

        @pl.when(to_ctx == ctx)
        def _():
            for step in range(1, n_pre):
                pl.when(pre >= step)(functools.partial(act, n_pre - step))

    def over_planes(first, last, loop, act):
        def plane(to_ctx, carry):
            loop(to_ctx, functools.partial(act, to_ctx))
            return carry

        lax.fori_loop(first, last, plane, 0)

    def send_query(to_ctx, step):
        pltpu.make_async_remote_copy(
            src_ref=outgoing.at[pre_at[step % n_pre]], dst_ref=q_in.at[ctx, pre], send_sem=q_send, recv_sem=q_recv.at[ctx],
            device_id=device(step, to_ctx), device_id_type=pl.DeviceIdType.LOGICAL,
        ).start()

    loads = [
        pltpu.make_async_copy(ids_hbm, ids, load_sem.at[2]),
        pltpu.make_async_copy(queries_hbm, queries, load_sem.at[3]),
        pltpu.make_async_copy(keys.at[0], k_raw, load_sem.at[0]),
        pltpu.make_async_copy(values.at[0], v_ones.at[:, pl.ds(0, DH)], load_sem.at[1]),
    ]
    for copy in loads:
        copy.start()
    barrier = pltpu.get_barrier_semaphore()

    over_planes(ctx, n_ctx, later_ones, lambda to_ctx, step: pl.semaphore_signal(
        barrier, inc=1, device_id=device(step, to_ctx), device_id_type=pl.DeviceIdType.LOGICAL
    ))

    @pl.when(rank > 0)
    def _():
        pl.semaphore_wait(barrier, rank)

    for half in range(2):
        @pl.when(in_half(pre, half))
        def _():
            over_planes(0, ctx + 1, earlier_ones, lambda to_ctx, step: pl.semaphore_signal(
                ready[half].at[ctx], inc=1, device_id=device(step, to_ctx), device_id_type=pl.DeviceIdType.LOGICAL
            ))

    for copy in loads[:2]:
        copy.wait()

    target_row, target_col = slot_targets(ids)
    r = iota((rows, LANES), 0)
    lane = iota((rows, LANES), 1)
    place = (jnp.broadcast_to(target_row, (rows, LANES)) == r // GROUP) & (r % GROUP == lane // n_req)
    by_head = jnp.concatenate([queries[:, e * DH:(e + 1) * DH] for e in range(GROUP)], axis=0)
    outgoing[...] = jnp.dot(
        jnp.where(place, 1.0, 0.0).astype(jnp.bfloat16), by_head, preferred_element_type=jnp.float32
    ).astype(jnp.bfloat16).reshape(n_pre, MSG, DH)

    pltpu.make_async_copy(outgoing.at[pre], q_in.at[ctx, pre], q_recv.at[ctx]).start()
    over_planes(0, ctx + 1, earlier_ones, send_query)
    v_ones[:, DH:] = jnp.ones((ctx_len, DH), jnp.bfloat16)

    def serve(to_ctx, carry):
        for half in range(2):
            whole = to_ctx > ctx
            if half:
                whole = whole | ((to_ctx == ctx) & in_half(pre, 0))
            later = (half + 1) * half_len - 1 - pre

            @pl.when(whole)
            def _():
                pl.semaphore_wait(ready[half].at[to_ctx], half_len)
                for step in range(1, n_pre + 1):
                    pl.when(in_half(pre_at[step % n_pre], half))(functools.partial(send_query, to_ctx, step))

            @pl.when((to_ctx == ctx) & in_half(pre, half) & (later > 0))
            def _():
                pl.semaphore_wait(ready[half].at[to_ctx], later)
                for step in range(1, half_len):
                    pl.when(pre + step < (half + 1) * half_len)(functools.partial(send_query, to_ctx, step))

        return carry

    lax.fori_loop(0, n_ctx, serve, 0)
    for copy in loads[2:]:
        copy.wait()
    own_lanes = iota((LANES, LANES), 1) == lax.rem(pre, per_tile) * MSG + iota((LANES, LANES), 0) % MSG
    n_steps = ctx_len // block_len

    def chunk_step(chunk, carry):
        pltpu.make_async_copy(q_in.at[chunk], q_in.at[chunk], q_recv.at[chunk]).wait()
        q = q_in[chunk].reshape(rows, DH)

        top = jnp.full((rows, LANES), -jnp.inf, jnp.float32)
        for piece in range(ctx_len // PIECE):
            span = slice(piece * PIECE, (piece + 1) * PIECE)
            s = lax.dot_general(q, k_raw[span], (((1,), (1,)), ((), ())), preferred_element_type=jnp.float32)
            scores[:, span] = s
            for i in range(PIECE // LANES):
                top = jnp.maximum(top, s[:, i * LANES:(i + 1) * LANES])
        top = jnp.max(top, axis=1, keepdims=True) * log_scale
        acc[...] = jnp.zeros(acc.shape, jnp.float32)

        def weight_step(j, carry):
            added = None
            for piece in range(block_len // PIECE):
                span = pl.ds(pl.multiple_of(j * block_len + piece * PIECE, PIECE), PIECE)
                p = jnp.exp2(scores[:, span] * log_scale - top).astype(jnp.bfloat16)
                more = jnp.dot(p, v_ones[span, :], preferred_element_type=jnp.float32)
                added = more if added is None else added + more
            acc[...] += added
            return carry

        lax.fori_loop(0, n_steps, weight_step, 0)
        denom = acc[:, DH:]
        lse = top + jnp.log2(denom)
        part[chunk] = (acc[:, :DH] / denom).astype(jnp.bfloat16).reshape(n_pre, MSG, DH)
        for h in range(rows // LANES):
            spread = jnp.where(own_lanes, lse[h * LANES:(h + 1) * LANES], 0.0)
            stat[chunk, h * per_tile:(h + 1) * per_tile] = jnp.sum(
                spread.reshape(per_tile, MSG, LANES), axis=1, keepdims=True
            )

        def send_part(step):
            to = pre_at[step]
            for src, dst, send_sem, recv_sem in (
                (part, part_in, part_send, part_recv), (stat, stat_in, stat_send, stat_recv)
            ):
                pltpu.make_async_remote_copy(
                    src_ref=src.at[chunk, to], dst_ref=dst.at[ctx, pre], send_sem=send_sem, recv_sem=recv_sem,
                    device_id=device(step, chunk), device_id_type=pl.DeviceIdType.LOGICAL,
                ).start()

        @pl.when(chunk == ctx)
        def _():
            pltpu.make_async_copy(part.at[chunk, pre], part_in.at[ctx, pre], part_recv).start()
            pltpu.make_async_copy(stat.at[chunk, pre], stat_in.at[ctx, pre], stat_recv).start()

        @pl.when(chunk != ctx)
        def _():
            send_part(0)

        for step in range(1, n_pre):
            send_part(step)
        return carry

    lax.fori_loop(0, n_ctx, chunk_step, 0)

    targets = jnp.concatenate([target_col] * GROUP, axis=0)
    r = iota((GROUP * n_req, rows), 0)
    lane = iota((GROUP * n_req, rows), 1)
    pick = (targets == lane // GROUP) & (r // n_req == lane % GROUP)
    pltpu.make_async_copy(stat_in, stat_in, stat_recv).wait()
    lses = [
        jnp.concatenate([
            jnp.sum(stat_in[chunk, h * per_tile:(h + 1) * per_tile], axis=0) for h in range(rows // LANES)
        ], axis=1)
        for chunk in range(n_ctx)
    ]
    highest = functools.reduce(jnp.maximum, lses)
    shares = [jnp.exp2(lse - highest) for lse in lses]
    total = functools.reduce(jnp.add, shares)
    pltpu.make_async_copy(part_in, part_in, part_recv).wait()
    answer = None
    for chunk in range(n_ctx):
        weight = jnp.where(pick, shares[chunk] / total, 0.0)
        coarse = weight.astype(jnp.bfloat16)
        fine = (weight - coarse.astype(jnp.float32)).astype(jnp.bfloat16)
        arrived = part_in[chunk].reshape(rows, DH)
        for term in (coarse, fine):
            more = jnp.dot(term, arrived, preferred_element_type=jnp.float32)
            answer = more if answer is None else answer + more
    answer = answer.astype(jnp.bfloat16)
    for e in range(GROUP):
        out[:, e * DH:(e + 1) * DH] = answer[e * n_req:(e + 1) * n_req]

    def sent(ref, sem):
        pltpu.make_async_copy(ref.at[pl.ds(1, n_ctx - 1)], ref.at[pl.ds(1, n_ctx - 1)], sem).wait()
        pltpu.make_async_copy(ref.at[0, pl.ds(1, n_pre - 1)], ref.at[0, pl.ds(1, n_pre - 1)], sem).wait()

    sent(q_in, q_send)
    sent(part, part_send)
    sent(stat, stat_send)


def body(queries, prefix_ids, keys, values):
    n_pre = lax.axis_size("prefix")
    n_ctx = lax.axis_size("ctx")
    ctx_len = keys.shape[1]
    rows = n_pre * MSG
    block_len = min(2048, ctx_len)
    f32, bf16 = jnp.float32, jnp.bfloat16
    vmem = pl.BlockSpec(memory_space=pltpu.VMEM)
    hbm = pl.BlockSpec(memory_space=pl.ANY)
    dma = pltpu.SemaphoreType.DMA
    return pl.pallas_call(
        functools.partial(kernel, n_pre, n_ctx, block_len),
        out_shape=jax.ShapeDtypeStruct(queries.shape, bf16),
        in_specs=[hbm, hbm, hbm, hbm],
        out_specs=vmem,
        scratch_shapes=[
            pltpu.VMEM(queries.shape, bf16),
            pltpu.VMEM((1, queries.shape[0]), jnp.int32),
            pltpu.VMEM((n_pre, MSG, DH), bf16),
            pltpu.VMEM((n_ctx, n_pre, MSG, DH), bf16),
            pltpu.VMEM((ctx_len, DH), bf16),
            pltpu.VMEM((ctx_len, 2 * DH), bf16),
            pltpu.VMEM((rows, ctx_len), f32),
            pltpu.VMEM((rows, 2 * DH), f32),
            pltpu.VMEM((n_ctx, n_pre, MSG, DH), bf16),
            pltpu.VMEM((n_ctx, n_pre, 1, LANES), f32),
            pltpu.VMEM((n_ctx, n_pre, MSG, DH), bf16),
            pltpu.VMEM((n_ctx, n_pre, 1, LANES), f32),
            pltpu.SemaphoreType.REGULAR((n_ctx,)), pltpu.SemaphoreType.REGULAR((n_ctx,)), dma((4,)), dma, dma((n_ctx,)), dma, dma, dma, dma,
        ],
        compiler_params=pltpu.CompilerParams(
            collective_id=0, has_side_effects=True, vmem_limit_bytes=VMEM_LIMIT
        ),
        cost_estimate=pl.CostEstimate(
            flops=4 * n_ctx * rows * ctx_len * DH, bytes_accessed=4 * ctx_len * DH,
            transcendentals=n_ctx * rows * ctx_len,
        ),
    )(queries, prefix_ids.reshape(1, -1), keys, values)


def solution(mesh):
    in_specs = (
        P(("prefix", "ctx"), "kvh"),
        P(("prefix", "ctx"), None),
        P("prefix", "ctx", "kvh"),
        P("prefix", "ctx", "kvh"),
    )
    out_specs = P(("prefix", "ctx"), "kvh")
    return jax.shard_map(body, mesh=mesh, in_specs=in_specs, out_specs=out_specs, check_vma=False)
```

```python
import functools
import math

import jax
import jax.numpy as jnp
from jax import lax
from jax.experimental import pallas as pl
from jax.experimental.pallas import tpu as pltpu
from jax.sharding import PartitionSpec as P

DH = 128
SEND_CAP = 2
GROUP = 8
VMEM_LIMIT = 63 * 1024 * 1024
LANES = 128
PIECE = 512
MSG = SEND_CAP * GROUP


def iota(shape, dim):
    return lax.broadcasted_iota(jnp.int32, shape, dim)


def slot_targets(ids_ref):
    n_req = ids_ref.shape[1]
    lane_req = iota((n_req, LANES), 1) % n_req
    row_req = iota((n_req, LANES), 0)
    row = jnp.concatenate([ids_ref[...]] * (LANES // n_req), axis=1)
    col = jnp.sum(jnp.where(iota((n_req, LANES), 1) == row_req, row, 0), axis=1, keepdims=True)
    same = col == row
    rank_row = jnp.sum(jnp.where(same & (row_req < lane_req), 1, 0), axis=0, keepdims=True)
    first = iota((n_req, LANES), 1) < row_req
    rank_col = jnp.sum(jnp.where(same & first, 1, 0), axis=1, keepdims=True)
    return row * SEND_CAP + rank_row, col * SEND_CAP + rank_col


def kernel(
    n_pre, n_ctx, block_len, queries_hbm, ids_hbm, keys, values, out,
    queries, ids, outgoing, q_in, k_raw, v_ones, scores, acc, part, stat, part_in, stat_in,
    ready_low, ready_high, load_sem, q_send, q_recv, part_send, part_recv, stat_send, stat_recv,
):
    n_req, features = queries.shape
    ctx_len = keys.shape[1]
    rows = n_pre * MSG
    per_tile = LANES // MSG
    pre = lax.axis_index("prefix")
    ctx = lax.axis_index("ctx")
    log_scale = DH ** (-0.5) * math.log2(math.e)

    kvh, n_kvh = lax.axis_index("kvh"), lax.axis_size("kvh")
    pre_at = [lax.rem(pre + step, n_pre) for step in range(n_pre)]
    pre_base = [to * (n_ctx * n_kvh) + kvh for to in pre_at]
    rank = ctx * n_pre + pre
    half_len = n_pre // 2
    ready = (ready_low, ready_high)

    def in_half(index, half):
        return index >= half_len if half else index < half_len

    def device(step, to_ctx):
        return pre_base[step % n_pre] + to_ctx * n_kvh

    def later_ones(to_ctx, act):
        @pl.when(to_ctx > ctx)
        def _():
            for step in range(1, n_pre + 1):
                act(step)

        @pl.when(to_ctx == ctx)
        def _():
            for step in range(1, n_pre):
                pl.when(pre + step < n_pre)(functools.partial(act, step))

    def earlier_ones(to_ctx, act):
        @pl.when(to_ctx < ctx)
        def _():
            for step in range(1, n_pre + 1):
                act(n_pre - step)

        @pl.when(to_ctx == ctx)
        def _():
            for step in range(1, n_pre):
                pl.when(pre >= step)(functools.partial(act, n_pre - step))

    def over_planes(first, last, loop, act):
        def plane(to_ctx, carry):
            loop(to_ctx, functools.partial(act, to_ctx))
            return carry

        lax.fori_loop(first, last, plane, 0)

    def send_query(to_ctx, step):
        pltpu.make_async_remote_copy(
            src_ref=outgoing.at[pre_at[step % n_pre]], dst_ref=q_in.at[ctx, pre], send_sem=q_send, recv_sem=q_recv.at[ctx],
            device_id=device(step, to_ctx), device_id_type=pl.DeviceIdType.LOGICAL,
        ).start()

    loads = [
        pltpu.make_async_copy(ids_hbm, ids, load_sem.at[2]),
        pltpu.make_async_copy(queries_hbm, queries, load_sem.at[3]),
        pltpu.make_async_copy(keys.at[0], k_raw, load_sem.at[0]),
        pltpu.make_async_copy(values.at[0], v_ones.at[:, pl.ds(0, DH)], load_sem.at[1]),
    ]
    for copy in loads:
        copy.start()
    barrier = pltpu.get_barrier_semaphore()

    over_planes(ctx, n_ctx, later_ones, lambda to_ctx, step: pl.semaphore_signal(
        barrier, inc=1, device_id=device(step, to_ctx), device_id_type=pl.DeviceIdType.LOGICAL
    ))

    @pl.when(rank > 0)
    def _():
        pl.semaphore_wait(barrier, rank)

    for half in range(2):
        @pl.when(in_half(pre, half))
        def _():
            over_planes(0, ctx + 1, earlier_ones, lambda to_ctx, step: pl.semaphore_signal(
                ready[half].at[ctx], inc=1, device_id=device(step, to_ctx), device_id_type=pl.DeviceIdType.LOGICAL
            ))

    for copy in loads[:2]:
        copy.wait()

    target_row, target_col = slot_targets(ids)
    r = iota((rows, LANES), 0)
    lane = iota((rows, LANES), 1)
    place = (jnp.broadcast_to(target_row, (rows, LANES)) == r // GROUP) & (r % GROUP == lane // n_req)
    by_head = jnp.concatenate([queries[:, e * DH:(e + 1) * DH] for e in range(GROUP)], axis=0)
    outgoing[...] = jnp.dot(
        jnp.where(place, 1.0, 0.0).astype(jnp.bfloat16), by_head, preferred_element_type=jnp.float32
    ).astype(jnp.bfloat16).reshape(n_pre, MSG, DH)

    pltpu.make_async_copy(outgoing.at[pre], q_in.at[ctx, pre], q_recv.at[ctx]).start()
    over_planes(0, ctx + 1, earlier_ones, send_query)
    v_ones[:, DH:] = jnp.ones((ctx_len, DH), jnp.bfloat16)

    def serve(to_ctx, carry):
        for half in range(2):
            whole = to_ctx > ctx
            if half:
                whole = whole | ((to_ctx == ctx) & in_half(pre, 0))
            later = (half + 1) * half_len - 1 - pre

            @pl.when(whole)
            def _():
                pl.semaphore_wait(ready[half].at[to_ctx], half_len)
                for step in range(1, n_pre + 1):
                    pl.when(in_half(pre_at[step % n_pre], half))(functools.partial(send_query, to_ctx, step))

            @pl.when((to_ctx == ctx) & in_half(pre, half) & (later > 0))
            def _():
                pl.semaphore_wait(ready[half].at[to_ctx], later)
                for step in range(1, half_len):
                    pl.when(pre + step < (half + 1) * half_len)(functools.partial(send_query, to_ctx, step))

        return carry

    lax.fori_loop(0, n_ctx, serve, 0)
    for copy in loads[2:]:
        copy.wait()
    own_lanes = iota((LANES, LANES), 1) == lax.rem(pre, per_tile) * MSG + iota((LANES, LANES), 0) % MSG
    n_steps = ctx_len // block_len

    def chunk_step(chunk, carry):
        pltpu.make_async_copy(q_in.at[chunk], q_in.at[chunk], q_recv.at[chunk]).wait()
        q = q_in[chunk].reshape(rows, DH)

        top = jnp.full((rows, LANES), -jnp.inf, jnp.float32)
        for piece in range(ctx_len // PIECE):
            span = slice(piece * PIECE, (piece + 1) * PIECE)
            s = lax.dot_general(q, k_raw[span], (((1,), (1,)), ((), ())), preferred_element_type=jnp.float32)
            scores[:, span] = s
            for i in range(PIECE // LANES):
                top = jnp.maximum(top, s[:, i * LANES:(i + 1) * LANES])
        top = jnp.max(top, axis=1, keepdims=True) * log_scale
        acc[...] = jnp.zeros(acc.shape, jnp.float32)

        def weight_step(j, carry):
            added = None
            for piece in range(block_len // PIECE):
                span = pl.ds(pl.multiple_of(j * block_len + piece * PIECE, PIECE), PIECE)
                p = jnp.exp2(scores[:, span] * log_scale - top).astype(jnp.bfloat16)
                more = jnp.dot(p, v_ones[span, :], preferred_element_type=jnp.float32)
                added = more if added is None else added + more
            acc[...] += added
            return carry

        lax.fori_loop(0, n_steps, weight_step, 0)
        denom = acc[:, DH:]
        lse = top + jnp.log2(denom)
        part[chunk] = (acc[:, :DH] / denom).astype(jnp.bfloat16).reshape(n_pre, MSG, DH)
        for h in range(rows // LANES):
            spread = jnp.where(own_lanes, lse[h * LANES:(h + 1) * LANES], 0.0)
            stat[chunk, h * per_tile:(h + 1) * per_tile] = jnp.sum(
                spread.reshape(per_tile, MSG, LANES), axis=1, keepdims=True
            )

        def send_part(step):
            to = lax.rem(pre + step, n_pre)
            number = to * (n_ctx * n_kvh) + kvh + chunk * n_kvh
            for src, dst, send_sem, recv_sem in (
                (part, part_in, part_send, part_recv), (stat, stat_in, stat_send, stat_recv)
            ):
                pltpu.make_async_remote_copy(
                    src_ref=src.at[chunk, to], dst_ref=dst.at[ctx, pre], send_sem=send_sem, recv_sem=recv_sem,
                    device_id=number, device_id_type=pl.DeviceIdType.LOGICAL,
                ).start()

        @pl.when(chunk == ctx)
        def _():
            pltpu.make_async_copy(part.at[chunk, pre], part_in.at[ctx, pre], part_recv).start()
            pltpu.make_async_copy(stat.at[chunk, pre], stat_in.at[ctx, pre], stat_recv).start()

        @pl.when(chunk != ctx)
        def _():
            send_part(0)

        lax.fori_loop(1, n_pre, lambda step, carry: (send_part(step), carry)[1], 0)
        return carry

    lax.fori_loop(0, n_ctx, chunk_step, 0)

    targets = jnp.concatenate([target_col] * GROUP, axis=0)
    r = iota((GROUP * n_req, rows), 0)
    lane = iota((GROUP * n_req, rows), 1)
    pick = (targets == lane // GROUP) & (r // n_req == lane % GROUP)
    pltpu.make_async_copy(stat_in, stat_in, stat_recv).wait()
    lses = [
        jnp.concatenate([
            jnp.sum(stat_in[chunk, h * per_tile:(h + 1) * per_tile], axis=0) for h in range(rows // LANES)
        ], axis=1)
        for chunk in range(n_ctx)
    ]
    highest = functools.reduce(jnp.maximum, lses)
    shares = [jnp.exp2(lse - highest) for lse in lses]
    total = functools.reduce(jnp.add, shares)
    pltpu.make_async_copy(part_in, part_in, part_recv).wait()
    answer = None
    for chunk in range(n_ctx):
        weight = jnp.where(pick, shares[chunk] / total, 0.0)
        coarse = weight.astype(jnp.bfloat16)
        fine = (weight - coarse.astype(jnp.float32)).astype(jnp.bfloat16)
        arrived = part_in[chunk].reshape(rows, DH)
        for term in (coarse, fine):
            more = jnp.dot(term, arrived, preferred_element_type=jnp.float32)
            answer = more if answer is None else answer + more
    answer = answer.astype(jnp.bfloat16)
    for e in range(GROUP):
        out[:, e * DH:(e + 1) * DH] = answer[e * n_req:(e + 1) * n_req]

    def sent(ref, sem):
        pltpu.make_async_copy(ref.at[pl.ds(1, n_ctx - 1)], ref.at[pl.ds(1, n_ctx - 1)], sem).wait()
        pltpu.make_async_copy(ref.at[0, pl.ds(1, n_pre - 1)], ref.at[0, pl.ds(1, n_pre - 1)], sem).wait()

    sent(q_in, q_send)
    sent(part, part_send)
    sent(stat, stat_send)


def body(queries, prefix_ids, keys, values):
    n_pre = lax.axis_size("prefix")
    n_ctx = lax.axis_size("ctx")
    ctx_len = keys.shape[1]
    rows = n_pre * MSG
    block_len = min(2048, ctx_len)
    f32, bf16 = jnp.float32, jnp.bfloat16
    vmem = pl.BlockSpec(memory_space=pltpu.VMEM)
    hbm = pl.BlockSpec(memory_space=pl.ANY)
    dma = pltpu.SemaphoreType.DMA
    return pl.pallas_call(
        functools.partial(kernel, n_pre, n_ctx, block_len),
        out_shape=jax.ShapeDtypeStruct(queries.shape, bf16),
        in_specs=[hbm, hbm, hbm, hbm],
        out_specs=vmem,
        scratch_shapes=[
            pltpu.VMEM(queries.shape, bf16),
            pltpu.VMEM((1, queries.shape[0]), jnp.int32),
            pltpu.VMEM((n_pre, MSG, DH), bf16),
            pltpu.VMEM((n_ctx, n_pre, MSG, DH), bf16),
            pltpu.VMEM((ctx_len, DH), bf16),
            pltpu.VMEM((ctx_len, 2 * DH), bf16),
            pltpu.VMEM((rows, ctx_len), f32),
            pltpu.VMEM((rows, 2 * DH), f32),
            pltpu.VMEM((n_ctx, n_pre, MSG, DH), bf16),
            pltpu.VMEM((n_ctx, n_pre, 1, LANES), f32),
            pltpu.VMEM((n_ctx, n_pre, MSG, DH), bf16),
            pltpu.VMEM((n_ctx, n_pre, 1, LANES), f32),
            pltpu.SemaphoreType.REGULAR((n_ctx,)), pltpu.SemaphoreType.REGULAR((n_ctx,)), dma((4,)), dma, dma((n_ctx,)), dma, dma, dma, dma,
        ],
        compiler_params=pltpu.CompilerParams(
            collective_id=0, has_side_effects=True, vmem_limit_bytes=VMEM_LIMIT
        ),
        cost_estimate=pl.CostEstimate(
            flops=4 * n_ctx * rows * ctx_len * DH, bytes_accessed=4 * ctx_len * DH,
            transcendentals=n_ctx * rows * ctx_len,
        ),
    )(queries, prefix_ids.reshape(1, -1), keys, values)


def solution(mesh):
    in_specs = (
        P(("prefix", "ctx"), "kvh"),
        P(("prefix", "ctx"), None),
        P("prefix", "ctx", "kvh"),
        P("prefix", "ctx", "kvh"),
    )
    out_specs = P(("prefix", "ctx"), "kvh")
    return jax.shard_map(body, mesh=mesh, in_specs=in_specs, out_specs=out_specs, check_vma=False)
```

```python
import functools
import math

import jax
import jax.numpy as jnp
from jax import lax
from jax.experimental import pallas as pl
from jax.experimental.pallas import tpu as pltpu
from jax.sharding import PartitionSpec as P

DH = 128
SEND_CAP = 2
GROUP = 8
VMEM_LIMIT = 63 * 1024 * 1024
LANES = 128
PIECE = 512
WIDE = 1024
MSG = SEND_CAP * GROUP


def iota(shape, dim):
    return lax.broadcasted_iota(jnp.int32, shape, dim)


def slot_targets(ids_ref):
    n_req = ids_ref.shape[1]
    lane_req = iota((n_req, LANES), 1) % n_req
    row_req = iota((n_req, LANES), 0)
    row = jnp.concatenate([ids_ref[...]] * (LANES // n_req), axis=1)
    col = jnp.sum(jnp.where(iota((n_req, LANES), 1) == row_req, row, 0), axis=1, keepdims=True)
    same = col == row
    rank_row = jnp.sum(jnp.where(same & (row_req < lane_req), 1, 0), axis=0, keepdims=True)
    first = iota((n_req, LANES), 1) < row_req
    rank_col = jnp.sum(jnp.where(same & first, 1, 0), axis=1, keepdims=True)
    return row * SEND_CAP + rank_row, col * SEND_CAP + rank_col


def kernel(
    n_pre, n_ctx, block_len, queries_hbm, ids_hbm, keys, values, out,
    queries, ids, outgoing, q_in, k_raw, v_ones, scores, acc, part, stat, part_in, stat_in,
    ready_low, ready_high, load_sem, q_send, q_recv, part_send, part_recv, stat_send, stat_recv,
):
    n_req, features = queries.shape
    ctx_len = keys.shape[1]
    rows = n_pre * MSG
    per_tile = LANES // MSG
    pre = lax.axis_index("prefix")
    ctx = lax.axis_index("ctx")
    log_scale = DH ** (-0.5) * math.log2(math.e)

    kvh, n_kvh = lax.axis_index("kvh"), lax.axis_size("kvh")
    pre_at = [lax.rem(pre + step, n_pre) for step in range(n_pre)]
    pre_base = [to * (n_ctx * n_kvh) + kvh for to in pre_at]
    rank = ctx * n_pre + pre
    half_len = n_pre // 2
    ready = (ready_low, ready_high)

    def in_half(index, half):
        return index >= half_len if half else index < half_len

    def device(step, to_ctx):
        return pre_base[step % n_pre] + to_ctx * n_kvh

    def later_ones(to_ctx, act):
        @pl.when(to_ctx > ctx)
        def _():
            for step in range(1, n_pre + 1):
                act(step)

        @pl.when(to_ctx == ctx)
        def _():
            for step in range(1, n_pre):
                pl.when(pre + step < n_pre)(functools.partial(act, step))

    def earlier_ones(to_ctx, act):
        @pl.when(to_ctx < ctx)
        def _():
            for step in range(1, n_pre + 1):
                act(n_pre - step)

        @pl.when(to_ctx == ctx)
        def _():
            for step in range(1, n_pre):
                pl.when(pre >= step)(functools.partial(act, n_pre - step))

    def over_planes(first, last, loop, act):
        def plane(to_ctx, carry):
            loop(to_ctx, functools.partial(act, to_ctx))
            return carry

        lax.fori_loop(first, last, plane, 0)

    def send_query(to_ctx, step):
        pltpu.make_async_remote_copy(
            src_ref=outgoing.at[pre_at[step % n_pre]], dst_ref=q_in.at[ctx, pre], send_sem=q_send, recv_sem=q_recv.at[ctx],
            device_id=device(step, to_ctx), device_id_type=pl.DeviceIdType.LOGICAL,
        ).start()

    loads = [
        pltpu.make_async_copy(ids_hbm, ids, load_sem.at[2]),
        pltpu.make_async_copy(queries_hbm, queries, load_sem.at[3]),
        pltpu.make_async_copy(keys.at[0], k_raw, load_sem.at[0]),
        pltpu.make_async_copy(values.at[0], v_ones.at[:, pl.ds(0, DH)], load_sem.at[1]),
    ]
    for copy in loads:
        copy.start()
    barrier = pltpu.get_barrier_semaphore()

    over_planes(ctx, n_ctx, later_ones, lambda to_ctx, step: pl.semaphore_signal(
        barrier, inc=1, device_id=device(step, to_ctx), device_id_type=pl.DeviceIdType.LOGICAL
    ))

    @pl.when(rank > 0)
    def _():
        pl.semaphore_wait(barrier, rank)

    for half in range(2):
        @pl.when(in_half(pre, half))
        def _():
            over_planes(0, ctx + 1, earlier_ones, lambda to_ctx, step: pl.semaphore_signal(
                ready[half].at[ctx], inc=1, device_id=device(step, to_ctx), device_id_type=pl.DeviceIdType.LOGICAL
            ))

    for copy in loads[:2]:
        copy.wait()

    target_row, target_col = slot_targets(ids)
    r = iota((rows, LANES), 0)
    lane = iota((rows, LANES), 1)
    place = (jnp.broadcast_to(target_row, (rows, LANES)) == r // GROUP) & (r % GROUP == lane // n_req)
    by_head = jnp.concatenate([queries[:, e * DH:(e + 1) * DH] for e in range(GROUP)], axis=0)
    outgoing[...] = jnp.dot(
        jnp.where(place, 1.0, 0.0).astype(jnp.bfloat16), by_head, preferred_element_type=jnp.float32
    ).astype(jnp.bfloat16).reshape(n_pre, MSG, DH)

    pltpu.make_async_copy(outgoing.at[pre], q_in.at[ctx, pre], q_recv.at[ctx]).start()
    over_planes(0, ctx + 1, earlier_ones, send_query)
    v_ones[:, DH:] = jnp.ones((ctx_len, DH), jnp.bfloat16)

    def serve(to_ctx, carry):
        for half in range(2):
            whole = to_ctx > ctx
            if half:
                whole = whole | ((to_ctx == ctx) & in_half(pre, 0))
            later = (half + 1) * half_len - 1 - pre

            @pl.when(whole)
            def _():
                pl.semaphore_wait(ready[half].at[to_ctx], half_len)
                for step in range(1, n_pre + 1):
                    pl.when(in_half(pre_at[step % n_pre], half))(functools.partial(send_query, to_ctx, step))

            @pl.when((to_ctx == ctx) & in_half(pre, half) & (later > 0))
            def _():
                pl.semaphore_wait(ready[half].at[to_ctx], later)
                for step in range(1, half_len):
                    pl.when(pre + step < (half + 1) * half_len)(functools.partial(send_query, to_ctx, step))

        return carry

    lax.fori_loop(0, n_ctx, serve, 0)
    for copy in loads[2:]:
        copy.wait()
    own_lanes = iota((LANES, LANES), 1) == lax.rem(pre, per_tile) * MSG + iota((LANES, LANES), 0) % MSG
    n_steps = ctx_len // block_len

    def chunk_step(chunk, carry):
        pltpu.make_async_copy(q_in.at[chunk], q_in.at[chunk], q_recv.at[chunk]).wait()
        q = q_in[chunk].reshape(rows, DH)

        top = jnp.full((rows, LANES), -jnp.inf, jnp.float32)
        for piece in range(ctx_len // PIECE):
            span = slice(piece * PIECE, (piece + 1) * PIECE)
            s = lax.dot_general(q, k_raw[span], (((1,), (1,)), ((), ())), preferred_element_type=jnp.float32)
            scores[:, span] = s
            for i in range(PIECE // LANES):
                top = jnp.maximum(top, s[:, i * LANES:(i + 1) * LANES])
        top = jnp.max(top, axis=1, keepdims=True) * log_scale
        acc[...] = jnp.zeros(acc.shape, jnp.float32)

        def weight_step(j, carry):
            added = None
            for piece in range(block_len // WIDE):
                span = pl.ds(pl.multiple_of(j * block_len + piece * WIDE, WIDE), WIDE)
                p = jnp.exp2(scores[:, span] * log_scale - top).astype(jnp.bfloat16)
                more = jnp.dot(p, v_ones[span, :], preferred_element_type=jnp.float32)
                added = more if added is None else added + more
            acc[...] += added
            return carry

        lax.fori_loop(0, n_steps, weight_step, 0)
        denom = acc[:, DH:]
        lse = top + jnp.log2(denom)
        part[chunk] = (acc[:, :DH] / denom).astype(jnp.bfloat16).reshape(n_pre, MSG, DH)
        for h in range(rows // LANES):
            spread = jnp.where(own_lanes, lse[h * LANES:(h + 1) * LANES], 0.0)
            stat[chunk, h * per_tile:(h + 1) * per_tile] = jnp.sum(
                spread.reshape(per_tile, MSG, LANES), axis=1, keepdims=True
            )

        def send_part(step):
            to = pre_at[step]
            for src, dst, send_sem, recv_sem in (
                (part, part_in, part_send, part_recv), (stat, stat_in, stat_send, stat_recv)
            ):
                pltpu.make_async_remote_copy(
                    src_ref=src.at[chunk, to], dst_ref=dst.at[ctx, pre], send_sem=send_sem, recv_sem=recv_sem,
                    device_id=device(step, chunk), device_id_type=pl.DeviceIdType.LOGICAL,
                ).start()

        @pl.when(chunk == ctx)
        def _():
            pltpu.make_async_copy(part.at[chunk, pre], part_in.at[ctx, pre], part_recv).start()
            pltpu.make_async_copy(stat.at[chunk, pre], stat_in.at[ctx, pre], stat_recv).start()

        @pl.when(chunk != ctx)
        def _():
            send_part(0)

        for step in range(1, n_pre):
            send_part(step)
        return carry

    lax.fori_loop(0, n_ctx, chunk_step, 0)

    targets = jnp.concatenate([target_col] * GROUP, axis=0)
    r = iota((GROUP * n_req, rows), 0)
    lane = iota((GROUP * n_req, rows), 1)
    pick = (targets == lane // GROUP) & (r // n_req == lane % GROUP)
    pltpu.make_async_copy(stat_in, stat_in, stat_recv).wait()
    lses = [
        jnp.concatenate([
            jnp.sum(stat_in[chunk, h * per_tile:(h + 1) * per_tile], axis=0) for h in range(rows // LANES)
        ], axis=1)
        for chunk in range(n_ctx)
    ]
    highest = functools.reduce(jnp.maximum, lses)
    shares = [jnp.exp2(lse - highest) for lse in lses]
    total = functools.reduce(jnp.add, shares)
    pltpu.make_async_copy(part_in, part_in, part_recv).wait()
    answer = None
    for chunk in range(n_ctx):
        weight = jnp.where(pick, shares[chunk] / total, 0.0)
        coarse = weight.astype(jnp.bfloat16)
        fine = (weight - coarse.astype(jnp.float32)).astype(jnp.bfloat16)
        arrived = part_in[chunk].reshape(rows, DH)
        for term in (coarse, fine):
            more = jnp.dot(term, arrived, preferred_element_type=jnp.float32)
            answer = more if answer is None else answer + more
    answer = answer.astype(jnp.bfloat16)
    for e in range(GROUP):
        out[:, e * DH:(e + 1) * DH] = answer[e * n_req:(e + 1) * n_req]

    def sent(ref, sem):
        pltpu.make_async_copy(ref.at[pl.ds(1, n_ctx - 1)], ref.at[pl.ds(1, n_ctx - 1)], sem).wait()
        pltpu.make_async_copy(ref.at[0, pl.ds(1, n_pre - 1)], ref.at[0, pl.ds(1, n_pre - 1)], sem).wait()

    sent(q_in, q_send)
    sent(part, part_send)
    sent(stat, stat_send)


def body(queries, prefix_ids, keys, values):
    n_pre = lax.axis_size("prefix")
    n_ctx = lax.axis_size("ctx")
    ctx_len = keys.shape[1]
    rows = n_pre * MSG
    block_len = min(2048, ctx_len)
    f32, bf16 = jnp.float32, jnp.bfloat16
    vmem = pl.BlockSpec(memory_space=pltpu.VMEM)
    hbm = pl.BlockSpec(memory_space=pl.ANY)
    dma = pltpu.SemaphoreType.DMA
    return pl.pallas_call(
        functools.partial(kernel, n_pre, n_ctx, block_len),
        out_shape=jax.ShapeDtypeStruct(queries.shape, bf16),
        in_specs=[hbm, hbm, hbm, hbm],
        out_specs=vmem,
        scratch_shapes=[
            pltpu.VMEM(queries.shape, bf16),
            pltpu.VMEM((1, queries.shape[0]), jnp.int32),
            pltpu.VMEM((n_pre, MSG, DH), bf16),
            pltpu.VMEM((n_ctx, n_pre, MSG, DH), bf16),
            pltpu.VMEM((ctx_len, DH), bf16),
            pltpu.VMEM((ctx_len, 2 * DH), bf16),
            pltpu.VMEM((rows, ctx_len), f32),
            pltpu.VMEM((rows, 2 * DH), f32),
            pltpu.VMEM((n_ctx, n_pre, MSG, DH), bf16),
            pltpu.VMEM((n_ctx, n_pre, 1, LANES), f32),
            pltpu.VMEM((n_ctx, n_pre, MSG, DH), bf16),
            pltpu.VMEM((n_ctx, n_pre, 1, LANES), f32),
            pltpu.SemaphoreType.REGULAR((n_ctx,)), pltpu.SemaphoreType.REGULAR((n_ctx,)), dma((4,)), dma, dma((n_ctx,)), dma, dma, dma, dma,
        ],
        compiler_params=pltpu.CompilerParams(
            collective_id=0, has_side_effects=True, vmem_limit_bytes=VMEM_LIMIT
        ),
        cost_estimate=pl.CostEstimate(
            flops=4 * n_ctx * rows * ctx_len * DH, bytes_accessed=4 * ctx_len * DH,
            transcendentals=n_ctx * rows * ctx_len,
        ),
    )(queries, prefix_ids.reshape(1, -1), keys, values)


def solution(mesh):
    in_specs = (
        P(("prefix", "ctx"), "kvh"),
        P(("prefix", "ctx"), None),
        P("prefix", "ctx", "kvh"),
        P("prefix", "ctx", "kvh"),
    )
    out_specs = P(("prefix", "ctx"), "kvh")
    return jax.shard_map(body, mesh=mesh, in_specs=in_specs, out_specs=out_specs, check_vma=False)
```
